256 devices in a mesh: dp: 16 (over z, core), seq: 16 (over x, y).
Axes of the slice: x: 4, y: 4, z: 8, core: 2. Of those that a mesh axis runs over, the one named last changes fastest.
Arguments:
- queries: bfloat16 [16, 2048, 4096], P('dp', 'seq'), may hold values from -6 to 6
- keys: bfloat16 [16, 2048, 4096], P('dp', 'seq'), may hold values from -6 to 6
- values: bfloat16 [16, 2048, 4096], P('dp', 'seq'), may hold values from -6 to 6
- cotangent: bfloat16 [16, 2048, 4096], P('dp', 'seq'), may hold values from -6 to 6
- query_gain: float32 [32, 128], replicated, may hold values from 0.1 to 1.9
- key_gain: float32 [32, 128], replicated, may hold values from 0.1 to 1.9
- block_ids: int32 [32, 8], replicated, may hold values from -1 to 31, as said below
Outputs:
- out: bfloat16 [16, 2048, 4096], P('dp', 'seq')
- query_grad: bfloat16 [16, 2048, 4096], P('dp', 'seq')
- key_grad: bfloat16 [16, 2048, 4096], P('dp', 'seq')
- value_grad: bfloat16 [16, 2048, 4096], P('dp', 'seq')
- query_gain_grad: float32 [32, 128], replicated
- key_gain_grad: float32 [32, 128], replicated
The draws below stay inside these ranges and needn't reach their ends.
Inputs may be any that keep to these rules, and one draw needn't show every extreme that they name: `block_ids`: every row block r lists block r, block 0 and block 31, two window slots for blocks r - 1 and r + 1 (set to -1 where such a block is missing or is block 0 or 31), and three further blocks; no block is listed twice in a row.
All inputs are finite; a program needn't handle non-finite values.
Results may differ from the reference program's by a relative error of at most 0.011.
Values may be sent and summed in bfloat16 or wider, within the bound.
No kernel may reach another device: no remote copies, remote signals or barrier semaphores. Data moves between devices by JAX's collectives and lax.ppermute only.
A program may use at most 128 MiB of HBM per device.

```python
import jax
import jax.numpy as jnp
from jax import lax

HEADS = 32
HEAD = 128
BLOCK = 64
SEQ_LEN = 2048
NB = 32
BATCH = 16


def draw_block_ids(key, part):
    rows = jnp.arange(NB, dtype=jnp.int32)
    last = NB - 1
    window = jnp.stack([rows - 1, rows, rows + 1], axis=1)
    window = jnp.where((window <= 0) | (window >= last), -1, window)
    global_pair = jnp.stack([jnp.zeros_like(rows), jnp.full_like(rows, last)], axis=1)
    columns = jnp.arange(NB, dtype=jnp.int32)
    nearby = jnp.abs(columns[None, :] - rows[:, None]) <= 1
    taken = nearby | (columns[None, :] == 0) | (columns[None, :] == last)
    random_part = jax.random.randint(key, (NB, NB), 0, 1 << 20, dtype=jnp.int32)
    ranking = jnp.where(taken, (1 << 30) + columns[None, :], random_part * NB + columns[None, :])
    picked = jnp.argsort(ranking, axis=1)[:, :3].astype(jnp.int32)
    return jnp.concatenate([window, global_pair, picked], axis=1).astype(jnp.int32)


def shard_levels(own_key, shape, pieces, smallest, largest):
    def one(axis_at, shards_of):
        heights = jax.random.uniform(jax.random.fold_in(jax.random.fold_in(own_key, 6), axis_at), (shards_of,), jnp.float32, smallest / len(pieces), largest / len(pieces))
        return jnp.repeat(jnp.exp(heights), shape[axis_at] // shards_of).reshape((-1,) + (1,) * (len(shape) - axis_at - 1))

    factor_of = one(*pieces[0])
    for cut in pieces[1:]:
        factor_of = factor_of * one(*cut)
    return factor_of


def normal_values(stream_key, shape, spread, limit, cuts=(), held_as=jnp.bfloat16):
    values = spread * jax.random.normal(stream_key, shape, jnp.float32)
    if cuts:
        values = values * shard_levels(stream_key, shape, cuts, -0.22, 0.18)
    return jnp.clip(values, -limit, limit).astype(held_as)


def setup_inputs(seed: int = 0) -> dict:
    arg_keys = jax.random.split(jax.random.key(seed), 8)
    queries = normal_values(arg_keys[0], (BATCH, SEQ_LEN, HEADS * HEAD), 1.0, 6.0, ((0, 16), (1, 16)))
    keys = normal_values(arg_keys[1], (BATCH, SEQ_LEN, HEADS * HEAD), 1.0, 6.0, ((0, 16), (1, 16)))
    values = normal_values(arg_keys[2], (BATCH, SEQ_LEN, HEADS * HEAD), 1.0, 6.0, ((0, 16), (1, 16)))
    cotangent = normal_values(arg_keys[3], (BATCH, SEQ_LEN, HEADS * HEAD), 1.0, 6.0, ((0, 16), (1, 16)))
    query_gain = jnp.clip(1.0 + 0.18 * jax.random.normal(arg_keys[4], (HEADS, HEAD), jnp.float32), 0.1, 1.9)
    key_gain = jnp.clip(1.0 + 0.18 * jax.random.normal(arg_keys[5], (HEADS, HEAD), jnp.float32), 0.1, 1.9)
    block_ids = draw_block_ids(jax.random.fold_in(arg_keys[7], 71), 0)
    return dict(queries=queries, keys=keys, values=values, cotangent=cotangent, query_gain=query_gain, key_gain=key_gain, block_ids=block_ids)


EPSILON = 1e-06

def stored(array):
    return lax.optimization_barrier(array.astype(jnp.bfloat16))

def normalize(values, gain):
    inverse = lax.rsqrt(lax.optimization_barrier(jnp.mean(values * values, axis=-1, keepdims=True)) + EPSILON)
    return values * inverse * gain

def gather_blocks(array, safe_ids):
    count, length, heads, depth = array.shape
    blocks = array.reshape(count, length // BLOCK, BLOCK, heads, depth)
    picked = blocks[:, safe_ids]
    return picked.reshape(count, length // BLOCK, safe_ids.shape[1] * BLOCK, heads, depth).astype(jnp.float32)

def probabilities(query_rows, keys_near, valid_wide):
    depth = query_rows.shape[-1]
    scores = jnp.einsum('brqhd,brshd->bhrqs', query_rows.astype(jnp.float32), keys_near) * depth ** (-0.5)
    raised = jnp.where(valid_wide[None, None, :, None, :], jnp.exp(scores), 0.0)
    return raised / lax.optimization_barrier(jnp.sum(raised, axis=4, keepdims=True))

def attend_backward(query, keys, values, cotangent, ids):
    count, length, heads, depth = query.shape
    nblocks = length // BLOCK
    valid = ids >= 0
    safe_ids = jnp.maximum(ids, 0).astype(jnp.int32)
    valid_wide = jnp.repeat(valid, BLOCK, axis=1)
    keys_near = gather_blocks(keys, safe_ids)
    values_near = gather_blocks(values, safe_ids)
    query_rows = query.reshape(count, nblocks, BLOCK, heads, depth).astype(jnp.float32)
    probs = probabilities(query_rows, keys_near, valid_wide)
    weights = stored(probs).astype(jnp.float32)
    mixed = jnp.einsum('bhrqs,brshd->brqhd', weights, values_near)
    output = stored(mixed.reshape(query.shape))
    grad_rows = cotangent.reshape(count, nblocks, BLOCK, heads, depth).astype(jnp.float32)
    delta = lax.optimization_barrier(jnp.sum(cotangent.astype(jnp.float32) * output.astype(jnp.float32), axis=-1))
    delta = jnp.transpose(delta.reshape(count, nblocks, BLOCK, heads), (0, 3, 1, 2))
    grad_weights = jnp.einsum('brqhd,brshd->bhrqs', grad_rows, values_near)
    grad_scores = stored(probs * (grad_weights - delta[..., None]) * depth ** (-0.5)).astype(jnp.float32)
    grad_query = jnp.einsum('bhrqs,brshd->brqhd', grad_scores, keys_near)
    grad_query = stored(grad_query.reshape(query.shape))
    key_terms = jnp.einsum('bhrqs,brqhd->rsbhd', grad_scores, query_rows)
    value_terms = jnp.einsum('bhrqs,brqhd->rsbhd', weights, grad_rows)
    targets = jnp.where(valid, ids, nblocks).reshape(-1).astype(jnp.int32)

    def collect(terms):
        flat = terms.reshape((nblocks * ids.shape[1], BLOCK) + terms.shape[2:])
        summed = jax.ops.segment_sum(flat, targets, num_segments=nblocks)
        return stored(jnp.transpose(summed, (2, 0, 1, 3, 4)).reshape(query.shape))
    return (output, grad_query, collect(key_terms), collect(value_terms))

def reference(queries, keys, values, cotangent, query_gain, key_gain, block_ids):

    def one_sequence(items):
        query_seq, key_seq, value_seq, grad_seq = items
        shape_heads = (1, SEQ_LEN, HEADS, HEAD)
        query_raw = query_seq.reshape(shape_heads).astype(jnp.float32)
        key_raw = key_seq.reshape(shape_heads).astype(jnp.float32)
        query_norm = stored(normalize(query_raw, query_gain))
        key_norm = stored(normalize(key_raw, key_gain))
        value_heads = value_seq.reshape(shape_heads)
        grad_heads = grad_seq.reshape(shape_heads)
        output, grad_qn, grad_kn, grad_value = attend_backward(query_norm, key_norm, value_heads, grad_heads, block_ids)
        _, pull_query = jax.vjp(normalize, query_raw, query_gain)
        query_back, query_gain_back = pull_query(grad_qn.astype(jnp.float32))
        _, pull_key = jax.vjp(normalize, key_raw, key_gain)
        key_back, key_gain_back = pull_key(grad_kn.astype(jnp.float32))
        flat = (SEQ_LEN, HEADS * HEAD)
        return (output.reshape(flat), query_back.astype(jnp.bfloat16).reshape(flat), key_back.astype(jnp.bfloat16).reshape(flat), grad_value.reshape(flat), query_gain_back, key_gain_back)
    results = lax.map(one_sequence, (queries, keys, values, cotangent))
    factor = (BATCH * SEQ_LEN) ** (-0.5)
    return (results[0], results[1], results[2], results[3], lax.optimization_barrier(jnp.sum(results[4], axis=0)) * factor, lax.optimization_barrier(jnp.sum(results[5], axis=0)) * factor)
```

```python
import functools

import jax
import jax.numpy as jnp
from jax import lax
from jax.experimental import pallas as pl
from jax.experimental.pallas import tpu as pltpu
from jax.sharding import PartitionSpec as P

HEADS = 32
HEAD = 128
BLOCK = 64
NB = 32
SLOTS = 8
SEQ = 16
CHUNKS = 2
TOK = 128
TOKENS = 2048
EPSILON = 1e-06
SCALE = HEAD**-0.5
LOG2E = 1.4426950408889634
EXTRA = 16
ROWS_OUT = 4 * TOK + EXTRA


def head_columns(chunk, s):
    return pl.ds(pl.multiple_of((chunk * SEQ + s) * HEAD, HEAD), HEAD)


def pack_kernel(chunk, q_ref, k_ref, v_ref, g_ref, send_ref, sem):
    @pl.loop(0, SEQ)
    def _(s):
        for a, ref in enumerate((q_ref, k_ref, v_ref, g_ref)):
            pltpu.make_async_copy(
                ref.at[0, :, head_columns(chunk, s)],
                send_ref.at[s, pl.ds(a * TOK, TOK), :],
                sem,
            ).start()

    pltpu.make_async_copy(send_ref, send_ref, sem).wait()


def pack(chunk, arrays):
    return pl.pallas_call(
        functools.partial(pack_kernel, chunk),
        out_shape=jax.ShapeDtypeStruct((SEQ, 4 * TOK, HEAD), jnp.bfloat16),
        in_specs=[pl.BlockSpec(memory_space=pl.ANY)] * 4,
        out_specs=pl.BlockSpec(memory_space=pl.ANY),
        scratch_shapes=[pltpu.SemaphoreType.DMA],
        cost_estimate=pl.CostEstimate(flops=0, bytes_accessed=4 << 20, transcendentals=0),
        name=f"pack{chunk}",
    )(*arrays)


def unpack_kernel(chunk, recv_ref, *refs):
    outs, sem = refs[-5:-1], refs[-1]

    @pl.loop(0, SEQ)
    def _(s):
        for a, ref in enumerate(outs):
            pltpu.make_async_copy(
                recv_ref.at[s, pl.ds(a * TOK, TOK), :],
                ref.at[0, :, head_columns(chunk, s)],
                sem,
            ).start()

    for ref in outs:
        half = ref.at[0, :, pl.ds(chunk * SEQ * HEAD, SEQ * HEAD)]
        pltpu.make_async_copy(half, half, sem).wait()


def unpack(chunk, recv, before):
    return pl.pallas_call(
        functools.partial(unpack_kernel, chunk),
        out_shape=(jax.ShapeDtypeStruct((1, TOK, HEADS * HEAD), jnp.bfloat16),) * 4,
        in_specs=[pl.BlockSpec(memory_space=pl.ANY)] * (1 + len(before)),
        out_specs=(pl.BlockSpec(memory_space=pl.ANY),) * 4,
        input_output_aliases={i + 1: i for i in range(len(before))},
        scratch_shapes=[pltpu.SemaphoreType.DMA],
        cost_estimate=pl.CostEstimate(flops=0, bytes_accessed=4 << 20, transcendentals=0),
        name=f"unpack{chunk}",
    )(recv, *before)


def dot(a, b, ca, cb):
    return lax.dot_general(
        a, b, (((ca,), (cb,)), ((), ())), preferred_element_type=jnp.float32
    )


def inverse_norm(x):
    return lax.rsqrt(jnp.mean(x * x, axis=-1, keepdims=True) + EPSILON)


def norm_backward(x, inverse, gain, grad):
    unit = x * inverse
    pulled = grad * gain
    along = jnp.mean(pulled * unit, axis=-1, keepdims=True)
    return inverse * (pulled - unit * along), grad * unit


def attend_kernel(ids_ref, gains_ref, recv_ref, back_ref, gain_ref, kn_ref, dk_ref, dv_ref, *, group):
    query_gain = gains_ref[0:1, :]
    key_gain = gains_ref[1:2, :]

    @pl.loop(0, SEQ)
    def _(s):
        x = recv_ref[s, TOK : 2 * TOK, :].astype(jnp.float32)
        rows = pl.ds(pl.multiple_of(s * TOK, TOK), TOK)
        kn_ref[rows, :] = (x * inverse_norm(x) * key_gain).astype(jnp.bfloat16)
        dk_ref[rows, :] = jnp.zeros((TOK, HEAD), jnp.float32)
        dv_ref[rows, :] = jnp.zeros((TOK, HEAD), jnp.float32)

    slot_of = lax.broadcasted_iota(jnp.int32, (1, SLOTS * BLOCK), 1) // BLOCK

    def one_row_block(r):
        src, at = r // 2, pl.multiple_of((r % 2) * BLOCK, BLOCK)
        places, tokens, valid = [], [], jnp.int32(0)
        for j in range(SLOTS):
            block = ids_ref[r, j]
            valid = valid | jnp.where(block >= 0, 1 << j, 0)
            block = jnp.maximum(block, 0)
            places.append(pl.ds(pl.multiple_of(block * BLOCK, BLOCK), BLOCK))
            tokens.append((block // 2, pl.multiple_of((block % 2) * BLOCK, BLOCK)))
        bias = jnp.where(((valid >> slot_of) & 1) == 1, 0.0, -1e30)
        x = recv_ref[src, pl.ds(at, BLOCK), :].astype(jnp.float32)
        inverse = inverse_norm(x)
        qn = (x * inverse * query_gain).astype(jnp.bfloat16)
        grad = recv_ref[src, pl.ds(3 * TOK + at, BLOCK), :]
        keys = jnp.concatenate([kn_ref[p, :] for p in places], axis=0)
        values = jnp.concatenate(
            [recv_ref[s, pl.ds(2 * TOK + o, BLOCK), :] for s, o in tokens], axis=0
        )
        scores = dot(qn, keys, 1, 1)
        raised = jnp.exp2(scores * (SCALE * LOG2E) + bias)
        probs = raised / jnp.sum(raised, axis=-1, keepdims=True)
        weights = probs.astype(jnp.bfloat16)
        out = dot(weights, values, 1, 0).astype(jnp.bfloat16)
        delta = jnp.sum(grad.astype(jnp.float32) * out.astype(jnp.float32), axis=-1, keepdims=True)
        grad_probs = dot(grad, values, 1, 1)
        grad_scores = (probs * (grad_probs - delta) * SCALE).astype(jnp.bfloat16)
        grad_qn = dot(grad_scores, keys, 1, 0).astype(jnp.bfloat16).astype(jnp.float32)
        query_grad, gain_term = norm_backward(x, inverse, query_gain, grad_qn)
        back_ref[src, pl.ds(at, BLOCK), :] = out
        back_ref[src, pl.ds(TOK + at, BLOCK), :] = query_grad.astype(jnp.bfloat16)
        key_terms = dot(grad_scores, qn, 0, 0)
        value_terms = dot(weights, grad, 0, 0)
        return places, key_terms, value_terms, gain_term.reshape(BLOCK // 8, 8, HEAD).sum(0)

    def several(i, total):
        done = [one_row_block(i * group + n) for n in range(group)]
        for places, key_terms, value_terms, gain_term in done:
            total = total + gain_term
            for j, p in enumerate(places):
                part = slice(j * BLOCK, (j + 1) * BLOCK)
                dk_ref[p, :] += key_terms[part]
                dv_ref[p, :] += value_terms[part]
        return total

    query_total = lax.fori_loop(0, NB // group, several, jnp.zeros((8, HEAD), jnp.float32))

    def finish(s, total):
        rows = pl.ds(pl.multiple_of(s * TOK, TOK), TOK)
        x = recv_ref[s, TOK : 2 * TOK, :].astype(jnp.float32)
        grad_kn = dk_ref[rows, :].astype(jnp.bfloat16).astype(jnp.float32)
        key_grad, gain_term = norm_backward(x, inverse_norm(x), key_gain, grad_kn)
        back_ref[s, 2 * TOK : 3 * TOK, :] = key_grad.astype(jnp.bfloat16)
        back_ref[s, 3 * TOK : 4 * TOK, :] = dv_ref[rows, :].astype(jnp.bfloat16)
        return total + gain_term.reshape(TOK // 8, 8, HEAD).sum(0)

    key_total = lax.fori_loop(0, SEQ, finish, jnp.zeros((8, HEAD), jnp.float32))
    gain_ref[0:1, :] = jnp.sum(query_total, axis=0, keepdims=True)
    gain_ref[1:2, :] = jnp.sum(key_total, axis=0, keepdims=True)


def attend(chunk, ids, gains, recv, group=2):
    return pl.pallas_call(
        functools.partial(attend_kernel, group=group),
        out_shape=(
            jax.ShapeDtypeStruct((SEQ, 4 * TOK, HEAD), jnp.bfloat16),
            jax.ShapeDtypeStruct((2, HEAD), jnp.float32),
        ),
        in_specs=[
            pl.BlockSpec(memory_space=pltpu.SMEM),
            pl.BlockSpec(memory_space=pltpu.VMEM),
            pl.BlockSpec(memory_space=pltpu.VMEM),
        ],
        out_specs=(
            pl.BlockSpec(memory_space=pltpu.VMEM),
            pl.BlockSpec(memory_space=pltpu.VMEM),
        ),
        scratch_shapes=[
            pltpu.VMEM((TOKENS, HEAD), jnp.bfloat16),
            pltpu.VMEM((TOKENS, HEAD), jnp.float32),
            pltpu.VMEM((TOKENS, HEAD), jnp.float32),
        ],
        compiler_params=pltpu.CompilerParams(vmem_limit_bytes=32 << 20),
        cost_estimate=pl.CostEstimate(
            flops=12 * 2 * NB * BLOCK * SLOTS * BLOCK * HEAD,
            bytes_accessed=4 << 20,
            transcendentals=NB * BLOCK * SLOTS * BLOCK,
        ),
        name=f"attend{chunk}",
    )(ids, gains, recv)


def swap(x, axis):
    return lax.all_to_all(x, axis, split_axis=0, concat_axis=0, tiled=True)


def on_device(queries, keys, values, cotangent, query_gain, key_gain, block_ids):
    arrays = (queries, keys, values, cotangent)
    s = lax.axis_index("seq")
    both = jnp.stack([query_gain, key_gain], axis=1)
    gains = [
        lax.dynamic_index_in_dim(both, c * SEQ + s, 0, keepdims=False) for c in range(CHUNKS)
    ]
    sent0 = pack(0, arrays)
    in0 = swap(sent0, "seq")
    sent1, in0 = lax.optimization_barrier((pack(1, arrays), in0))
    in1 = swap(sent1, "seq")
    back0, gain0 = attend(0, block_ids, gains[0], in0)
    back0, in1 = lax.optimization_barrier((back0, in1))
    out0 = swap(back0, "seq")
    back1, gain1 = attend(1, block_ids, gains[1], in1)
    back1, out0 = lax.optimization_barrier((back1, out0))
    out1 = swap(back1, "seq")
    done = unpack(0, out0, ())
    done = unpack(1, out1, tuple(done))
    part = jnp.stack([gain0, gain1])
    part = jnp.sum(swap(jnp.broadcast_to(part[None], (SEQ, 2, 2, HEAD)), "dp"), axis=0)
    every = swap(jnp.broadcast_to(part[None], (SEQ, 2, 2, HEAD)), "seq")
    factor = (TOKENS * lax.axis_size("dp")) ** -0.5
    every = jnp.transpose(every, (2, 1, 0, 3)).reshape(2, HEADS, HEAD) * factor
    return (*done, every[0], every[1])


def solution(mesh):
    rows = P("dp", "seq", None)
    return jax.shard_map(
        on_device,
        mesh=mesh,
        in_specs=(rows, rows, rows, rows, P(), P(), P()),
        out_specs=(rows, rows, rows, rows, P(), P()),
        check_vma=False,
    )
```

```python
import functools

import jax
import jax.numpy as jnp
from jax import lax
from jax.experimental import pallas as pl
from jax.experimental.pallas import tpu as pltpu
from jax.sharding import PartitionSpec as P

HEADS = 32
HEAD = 128
BLOCK = 64
NB = 32
SLOTS = 8
SEQ = 16
CHUNKS = 2
TOK = 128
TOKENS = 2048
EPSILON = 1e-06
SCALE = HEAD**-0.5
LOG2E = 1.4426950408889634
AT_ONCE = 8


def pack_kernel(q_ref, k_ref, v_ref, g_ref, send_ref):
    for a, ref in enumerate((q_ref, k_ref, v_ref, g_ref)):
        for n in range(AT_ONCE):
            send_ref[n, a * TOK : (a + 1) * TOK, :] = ref[0, :, n * HEAD : (n + 1) * HEAD]


def pack(chunk, arrays):
    steps = SEQ // AT_ONCE
    return pl.pallas_call(
        pack_kernel,
        grid=(steps,),
        out_shape=jax.ShapeDtypeStruct((SEQ, 4 * TOK, HEAD), jnp.bfloat16),
        in_specs=[pl.BlockSpec((1, TOK, AT_ONCE * HEAD), lambda i: (0, 0, chunk * steps + i))] * 4,
        out_specs=pl.BlockSpec((AT_ONCE, 4 * TOK, HEAD), lambda i: (i, 0, 0)),
        cost_estimate=pl.CostEstimate(flops=0, bytes_accessed=8 << 20, transcendentals=0),
        name=f"pack{chunk}",
    )(*arrays)


def unpack_kernel(recv_ref, *refs):
    first = pl.program_id(0) * AT_ONCE
    for a, ref in enumerate(refs[-4:]):
        for n in range(AT_ONCE):
            ref[0, :, n * HEAD : (n + 1) * HEAD] = recv_ref[first + n, a * TOK : (a + 1) * TOK, :]


def unpack(chunk, recv, before):
    steps = SEQ // AT_ONCE
    return pl.pallas_call(
        unpack_kernel,
        grid=(steps,),
        out_shape=(jax.ShapeDtypeStruct((1, TOK, HEADS * HEAD), jnp.bfloat16),) * 4,
        in_specs=[pl.BlockSpec(memory_space=pltpu.VMEM)]
        + [pl.BlockSpec(memory_space=pl.ANY)] * len(before),
        out_specs=(pl.BlockSpec((1, TOK, AT_ONCE * HEAD), lambda i: (0, 0, chunk * steps + i)),) * 4,
        input_output_aliases={i + 1: i for i in range(len(before))},
        cost_estimate=pl.CostEstimate(flops=0, bytes_accessed=8 << 20, transcendentals=0),
        name=f"unpack{chunk}",
    )(recv, *before)


def dot(a, b, ca, cb):
    return lax.dot_general(
        a, b, (((ca,), (cb,)), ((), ())), preferred_element_type=jnp.float32
    )


def inverse_norm(x):
    return lax.rsqrt(jnp.mean(x * x, axis=-1, keepdims=True) + EPSILON)


def norm_backward(x, inverse, gain, grad):
    unit = x * inverse
    pulled = grad * gain
    along = jnp.mean(pulled * unit, axis=-1, keepdims=True)
    return inverse * (pulled - unit * along), grad * unit


def attend_kernel(ids_ref, gains_ref, recv_ref, back_ref, gain_ref, kv_ref, sum_ref, *, group):
    query_gain = gains_ref[0:1, :]
    key_gain = gains_ref[1:2, :]

    @pl.loop(0, SEQ, unroll=4)
    def _(s):
        x = recv_ref[s, TOK : 2 * TOK, :].astype(jnp.float32)
        rows = pl.ds(pl.multiple_of(s * TOK, TOK), TOK)
        kv_ref[rows, :HEAD] = (x * inverse_norm(x) * key_gain).astype(jnp.bfloat16)
        kv_ref[rows, HEAD:] = recv_ref[s, 2 * TOK : 3 * TOK, :]
        sum_ref[rows, :] = jnp.zeros((TOK, 2 * HEAD), jnp.float32)

    slot_of = lax.broadcasted_iota(jnp.int32, (1, SLOTS * BLOCK), 1) // BLOCK
    zeros = jnp.zeros((BLOCK, HEAD), jnp.bfloat16)

    def one_row_block(r):
        src, at = r // 2, pl.multiple_of((r % 2) * BLOCK, BLOCK)
        places, valid = [], jnp.int32(0)
        for j in range(SLOTS):
            block = ids_ref[r, j]
            valid = valid | jnp.where(block >= 0, 1 << j, 0)
            places.append(pl.ds(pl.multiple_of(jnp.maximum(block, 0) * BLOCK, BLOCK), BLOCK))
        bias = jnp.where(((valid >> slot_of) & 1) == 1, 0.0, -1e30)
        x = recv_ref[src, pl.ds(at, BLOCK), :].astype(jnp.float32)
        inverse = inverse_norm(x)
        qn = (x * inverse * query_gain).astype(jnp.bfloat16)
        grad = recv_ref[src, pl.ds(3 * TOK + at, BLOCK), :]
        apart = jnp.concatenate(
            [jnp.concatenate([qn, zeros], axis=1), jnp.concatenate([zeros, grad], axis=1)], axis=0
        )
        near = jnp.concatenate([kv_ref[p, :] for p in places], axis=0)
        products = dot(apart, near, 1, 1)
        grad_probs = products[BLOCK:]
        raised = jnp.exp2(products[:BLOCK] * (SCALE * LOG2E) + bias)
        inverse_sum = 1.0 / jnp.sum(raised, axis=-1, keepdims=True)
        delta = jnp.sum(raised * grad_probs, axis=-1, keepdims=True) * inverse_sum
        weights = (raised * inverse_sum).astype(jnp.bfloat16)
        grad_scores = (raised * ((grad_probs - delta) * (inverse_sum * SCALE))).astype(jnp.bfloat16)
        both = jnp.concatenate([grad_scores, weights], axis=0)
        mixed = dot(both, near, 1, 0)
        grad_qn = mixed[:BLOCK, :HEAD].astype(jnp.bfloat16).astype(jnp.float32)
        query_grad, gain_term = norm_backward(x, inverse, query_gain, grad_qn)
        back_ref[src, pl.ds(at, BLOCK), :] = mixed[BLOCK:, HEAD:].astype(jnp.bfloat16)
        back_ref[src, pl.ds(TOK + at, BLOCK), :] = query_grad.astype(jnp.bfloat16)
        terms = dot(both, apart, 0, 0)
        return places, terms, gain_term.reshape(BLOCK // 8, 8, HEAD).sum(0)

    def several(i, total):
        done = [one_row_block(i * group + n) for n in range(group)]
        for places, terms, gain_term in done:
            total = total + gain_term
            for j, p in enumerate(places):
                sum_ref[p, :] += terms[j * BLOCK : (j + 1) * BLOCK]
        return total

    query_total = lax.fori_loop(0, NB // group, several, jnp.zeros((8, HEAD), jnp.float32))

    def finish(s, total):
        rows = pl.ds(pl.multiple_of(s * TOK, TOK), TOK)
        x = recv_ref[s, TOK : 2 * TOK, :].astype(jnp.float32)
        grad_kn = sum_ref[rows, :HEAD].astype(jnp.bfloat16).astype(jnp.float32)
        key_grad, gain_term = norm_backward(x, inverse_norm(x), key_gain, grad_kn)
        back_ref[s, 2 * TOK : 3 * TOK, :] = key_grad.astype(jnp.bfloat16)
        back_ref[s, 3 * TOK : 4 * TOK, :] = sum_ref[rows, HEAD:].astype(jnp.bfloat16)
        return total + gain_term.reshape(TOK // 8, 8, HEAD).sum(0)

    key_total = lax.fori_loop(0, SEQ, finish, jnp.zeros((8, HEAD), jnp.float32), unroll=4)
    gain_ref[0:1, :] = jnp.sum(query_total, axis=0, keepdims=True)
    gain_ref[1:2, :] = jnp.sum(key_total, axis=0, keepdims=True)


def attend(chunk, ids, gains, recv, group=4):
    return pl.pallas_call(
        functools.partial(attend_kernel, group=group),
        out_shape=(
            jax.ShapeDtypeStruct((SEQ, 4 * TOK, HEAD), jnp.bfloat16),
            jax.ShapeDtypeStruct((2, HEAD), jnp.float32),
        ),
        in_specs=[
            pl.BlockSpec(memory_space=pltpu.SMEM),
            pl.BlockSpec(memory_space=pltpu.VMEM),
            pl.BlockSpec(memory_space=pltpu.VMEM),
        ],
        out_specs=(
            pl.BlockSpec(memory_space=pltpu.VMEM),
            pl.BlockSpec(memory_space=pltpu.VMEM),
        ),
        scratch_shapes=[
            pltpu.VMEM((TOKENS, 2 * HEAD), jnp.bfloat16),
            pltpu.VMEM((TOKENS, 2 * HEAD), jnp.float32),
        ],
        compiler_params=pltpu.CompilerParams(vmem_limit_bytes=32 << 20),
        cost_estimate=pl.CostEstimate(
            flops=25_000_000_000,
            bytes_accessed=4 << 20,
            transcendentals=NB * BLOCK * SLOTS * BLOCK,
        ),
        name=f"attend{chunk}",
    )(ids, gains, recv)


def swap(x, axis):
    return lax.all_to_all(x, axis, split_axis=0, concat_axis=0, tiled=True)


def summed(x, axis):
    size, step = lax.axis_size(axis), 1
    while step < size:
        x = x + lax.ppermute(x, axis, [(i, i ^ step) for i in range(size)])
        step *= 2
    return x


def on_device(queries, keys, values, cotangent, query_gain, key_gain, block_ids):
    arrays = (queries, keys, values, cotangent)
    s = lax.axis_index("seq")
    both = jnp.stack([query_gain, key_gain], axis=1)
    gains = [
        lax.dynamic_index_in_dim(both, c * SEQ + s, 0, keepdims=False) for c in range(CHUNKS)
    ]
    sent0 = pack(0, arrays)
    in0 = swap(sent0, "seq")
    sent1, in0 = lax.optimization_barrier((pack(1, arrays), in0))
    in1 = swap(sent1, "seq")
    back0, gain0 = attend(0, block_ids, gains[0], in0)
    back0, in1 = lax.optimization_barrier((back0, in1))
    out0 = swap(back0, "seq")
    back1, gain1 = attend(1, block_ids, gains[1], in1)
    back1, gain1, out0 = lax.optimization_barrier((back1, gain1, out0))
    out1 = swap(back1, "seq")
    done = unpack(0, out0, ())
    done = unpack(1, out1, tuple(done))
    part = jnp.concatenate([gain0, gain1], axis=0)
    part = summed(part, "dp")
    mine = lax.broadcasted_iota(jnp.int32, (SEQ, 1, 1), 0) == s
    every = summed(jnp.where(mine, part[None], 0.0), "seq")
    factor = (TOKENS * lax.axis_size("dp")) ** -0.5
    every = jnp.transpose(every.reshape(SEQ, CHUNKS, 2, HEAD), (2, 1, 0, 3)) * factor
    every = every.reshape(2, HEADS, HEAD)
    return (*done, every[0], every[1])


def solution(mesh):
    rows = P("dp", "seq", None)
    return jax.shard_map(
        on_device,
        mesh=mesh,
        in_specs=(rows, rows, rows, rows, P(), P(), P()),
        out_specs=(rows, rows, rows, rows, P(), P()),
        check_vma=False,
    )
```

```python
import functools

import jax
import jax.numpy as jnp
from jax import lax
from jax.experimental import pallas as pl
from jax.experimental.pallas import tpu as pltpu
from jax.sharding import PartitionSpec as P

HEADS = 32
HEAD = 128
BLOCK = 64
NB = 32
SLOTS = 8
SEQ = 16
CHUNKS = 2
TOK = 128
TOKENS = 2048
EPSILON = 1e-06
SCALE = HEAD**-0.5
LOG2E = 1.4426950408889634
AT_ONCE = 8


def pack_kernel(q_ref, k_ref, v_ref, g_ref, send_ref):
    for a, ref in enumerate((q_ref, k_ref, v_ref, g_ref)):
        for n in range(AT_ONCE):
            send_ref[n, a * TOK : (a + 1) * TOK, :] = ref[0, :, n * HEAD : (n + 1) * HEAD]


def pack(chunk, arrays):
    steps = SEQ // AT_ONCE
    return pl.pallas_call(
        pack_kernel,
        grid=(steps,),
        out_shape=jax.ShapeDtypeStruct((SEQ, 4 * TOK, HEAD), jnp.bfloat16),
        in_specs=[pl.BlockSpec((1, TOK, AT_ONCE * HEAD), lambda i: (0, 0, chunk * steps + i))] * 4,
        out_specs=pl.BlockSpec((AT_ONCE, 4 * TOK, HEAD), lambda i: (i, 0, 0)),
        cost_estimate=pl.CostEstimate(flops=0, bytes_accessed=8 << 20, transcendentals=0),
        name=f"pack{chunk}",
    )(*arrays)


def unpack_kernel(recv_ref, *refs):
    first = pl.program_id(0) * AT_ONCE
    for a, ref in enumerate(refs[-4:]):
        for n in range(AT_ONCE):
            ref[0, :, n * HEAD : (n + 1) * HEAD] = recv_ref[first + n, a * TOK : (a + 1) * TOK, :]


def unpack(chunk, recv, before):
    steps = SEQ // AT_ONCE
    return pl.pallas_call(
        unpack_kernel,
        grid=(steps,),
        out_shape=(jax.ShapeDtypeStruct((1, TOK, HEADS * HEAD), jnp.bfloat16),) * 4,
        in_specs=[pl.BlockSpec(memory_space=pltpu.VMEM)]
        + [pl.BlockSpec(memory_space=pl.ANY)] * len(before),
        out_specs=(pl.BlockSpec((1, TOK, AT_ONCE * HEAD), lambda i: (0, 0, chunk * steps + i)),) * 4,
        input_output_aliases={i + 1: i for i in range(len(before))},
        compiler_params=pltpu.CompilerParams(vmem_limit_bytes=24 << 20),
        cost_estimate=pl.CostEstimate(flops=0, bytes_accessed=8 << 20, transcendentals=0),
        name=f"unpack{chunk}",
    )(recv, *before)


def dot(a, b, ca, cb):
    return lax.dot_general(
        a, b, (((ca,), (cb,)), ((), ())), preferred_element_type=jnp.float32
    )


def inverse_norm(x):
    return lax.rsqrt(jnp.mean(x * x, axis=-1, keepdims=True) + EPSILON)


def norm_backward(x, inverse, gain, grad):
    unit = x * inverse
    pulled = grad * gain
    along = jnp.mean(pulled * unit, axis=-1, keepdims=True)
    return inverse * (pulled - unit * along), grad * unit


def attend_kernel(
    ids_ref, gains_ref, recv_ref, back_ref, gain_ref, kv_ref, qg_ref, sum_ref, prod_a, prod_b, mix_a, mix_b, *, group
):
    query_gain = gains_ref[0:1, :]
    key_gain = gains_ref[1:2, :]
    prods, mixes = (prod_a, prod_b), (mix_a, mix_b)
    units = NB // group
    zeros = jnp.zeros((BLOCK, HEAD), jnp.bfloat16)

    @pl.loop(0, SEQ, unroll=4)
    def _(s):
        rows = pl.ds(pl.multiple_of(s * TOK, TOK), TOK)
        x = recv_ref[s, TOK : 2 * TOK, :].astype(jnp.float32)
        kv_ref[rows, :HEAD] = (x * inverse_norm(x) * key_gain).astype(jnp.bfloat16)
        kv_ref[rows, HEAD:] = recv_ref[s, 2 * TOK : 3 * TOK, :]
        sum_ref[rows, :] = jnp.zeros((TOK, 2 * HEAD), jnp.float32)
        x = recv_ref[s, :TOK, :].astype(jnp.float32)
        qn = (x * inverse_norm(x) * query_gain).astype(jnp.bfloat16)
        grad = recv_ref[s, 3 * TOK : 4 * TOK, :]
        for h in range(2):
            part = slice(h * BLOCK, (h + 1) * BLOCK)
            qg_ref[2 * s + h, :BLOCK, :HEAD] = qn[part]
            qg_ref[2 * s + h, :BLOCK, HEAD:] = zeros
            qg_ref[2 * s + h, BLOCK:, :HEAD] = zeros
            qg_ref[2 * s + h, BLOCK:, HEAD:] = grad[part]

    slot_of = lax.broadcasted_iota(jnp.int32, (1, SLOTS * BLOCK), 1) // BLOCK

    def places_of(r):
        blocks = [jnp.maximum(ids_ref[r, j], 0) for j in range(SLOTS)]
        return [pl.ds(pl.multiple_of(b * BLOCK, BLOCK), BLOCK) for b in blocks]

    def near_of(r):
        return jnp.concatenate([kv_ref[p, :] for p in places_of(r)], axis=0)

    def multiply(t, at):
        for n in range(group):
            r = t * group + n
            prods[at][n] = dot(qg_ref[r], near_of(r), 1, 1)

    def weigh(t, at):
        for n in range(group):
            r = t * group + n
            valid = jnp.int32(0)
            for j in range(SLOTS):
                valid = valid | jnp.where(ids_ref[r, j] >= 0, 1 << j, 0)
            bias = jnp.where(((valid >> slot_of) & 1) == 1, 0.0, -1e30)
            grad_probs = prods[at][n, BLOCK:, :]
            raised = jnp.exp2(prods[at][n, :BLOCK, :] * (SCALE * LOG2E) + bias)
            inverse_sum = 1.0 / jnp.sum(raised, axis=-1, keepdims=True)
            delta = jnp.sum(raised * grad_probs, axis=-1, keepdims=True) * inverse_sum
            mixes[at][n, BLOCK:, :] = (raised * inverse_sum).astype(jnp.bfloat16)
            grad_scores = raised * ((grad_probs - delta) * (inverse_sum * SCALE))
            mixes[at][n, :BLOCK, :] = grad_scores.astype(jnp.bfloat16)

    def spread(t, at, total):
        for n in range(group):
            r = t * group + n
            src, first = r // 2, pl.multiple_of((r % 2) * BLOCK, BLOCK)
            mixed = dot(mixes[at][n], near_of(r), 1, 0)
            x = recv_ref[src, pl.ds(first, BLOCK), :].astype(jnp.float32)
            grad_qn = mixed[:BLOCK, :HEAD].astype(jnp.bfloat16).astype(jnp.float32)
            query_grad, gain_term = norm_backward(x, inverse_norm(x), query_gain, grad_qn)
            back_ref[src, pl.ds(first, BLOCK), :] = mixed[BLOCK:, HEAD:].astype(jnp.bfloat16)
            back_ref[src, pl.ds(TOK + first, BLOCK), :] = query_grad.astype(jnp.bfloat16)
            total = total + gain_term.reshape(BLOCK // 8, 8, HEAD).sum(0)
            terms = dot(mixes[at][n], qg_ref[r], 0, 0)
            for j, p in enumerate(places_of(r)):
                sum_ref[p, :] += terms[j * BLOCK : (j + 1) * BLOCK]
        return total

    def step(t, at, total):
        multiply(t, at)
        weigh(t - 1, 1 - at)
        return spread(t - 2, at, total)

    def two_steps(i, total):
        return step(2 * i + 1, 1, step(2 * i, 0, total))

    multiply(0, 0)
    multiply(1, 1)
    weigh(0, 0)
    query_total = lax.fori_loop(1, units // 2, two_steps, jnp.zeros((8, HEAD), jnp.float32))
    weigh(units - 1, 1)
    query_total = spread(units - 2, 0, query_total)
    query_total = spread(units - 1, 1, query_total)

    def finish(s, total):
        rows = pl.ds(pl.multiple_of(s * TOK, TOK), TOK)
        x = recv_ref[s, TOK : 2 * TOK, :].astype(jnp.float32)
        grad_kn = sum_ref[rows, :HEAD].astype(jnp.bfloat16).astype(jnp.float32)
        key_grad, gain_term = norm_backward(x, inverse_norm(x), key_gain, grad_kn)
        back_ref[s, 2 * TOK : 3 * TOK, :] = key_grad.astype(jnp.bfloat16)
        back_ref[s, 3 * TOK : 4 * TOK, :] = sum_ref[rows, HEAD:].astype(jnp.bfloat16)
        return total + gain_term.reshape(TOK // 8, 8, HEAD).sum(0)

    key_total = lax.fori_loop(0, SEQ, finish, jnp.zeros((8, HEAD), jnp.float32), unroll=4)
    gain_ref[0:1, :] = jnp.sum(query_total, axis=0, keepdims=True)
    gain_ref[1:2, :] = jnp.sum(key_total, axis=0, keepdims=True)


def attend(chunk, ids, gains, recv, group=2):
    return pl.pallas_call(
        functools.partial(attend_kernel, group=group),
        out_shape=(
            jax.ShapeDtypeStruct((SEQ, 4 * TOK, HEAD), jnp.bfloat16),
            jax.ShapeDtypeStruct((2, HEAD), jnp.float32),
        ),
        in_specs=[
            pl.BlockSpec(memory_space=pltpu.SMEM),
            pl.BlockSpec(memory_space=pltpu.VMEM),
            pl.BlockSpec(memory_space=pltpu.VMEM),
        ],
        out_specs=(
            pl.BlockSpec(memory_space=pltpu.VMEM),
            pl.BlockSpec(memory_space=pltpu.VMEM),
        ),
        scratch_shapes=[
            pltpu.VMEM((TOKENS, 2 * HEAD), jnp.bfloat16),
            pltpu.VMEM((NB, 2 * BLOCK, 2 * HEAD), jnp.bfloat16),
            pltpu.VMEM((TOKENS, 2 * HEAD), jnp.float32),
            pltpu.VMEM((group, 2 * BLOCK, SLOTS * BLOCK), jnp.float32),
            pltpu.VMEM((group, 2 * BLOCK, SLOTS * BLOCK), jnp.float32),
            pltpu.VMEM((group, 2 * BLOCK, SLOTS * BLOCK), jnp.bfloat16),
            pltpu.VMEM((group, 2 * BLOCK, SLOTS * BLOCK), jnp.bfloat16),
        ],
        compiler_params=pltpu.CompilerParams(vmem_limit_bytes=32 << 20),
        cost_estimate=pl.CostEstimate(
            flops=25_000_000_000,
            bytes_accessed=4 << 20,
            transcendentals=NB * BLOCK * SLOTS * BLOCK,
        ),
        name=f"attend{chunk}",
    )(ids, gains, recv)


def swap(x, axis):
    return lax.all_to_all(x, axis, split_axis=0, concat_axis=0, tiled=True)


def summed(x, axis, steps):
    size = lax.axis_size(axis)
    for step in steps:
        x = x + lax.ppermute(x, axis, [(i, i ^ step) for i in range(size)])
    return x


def on_device(queries, keys, values, cotangent, query_gain, key_gain, block_ids):
    arrays = (queries, keys, values, cotangent)
    s = lax.axis_index("seq")
    both = jnp.stack([query_gain, key_gain], axis=1)
    gains = [
        lax.dynamic_index_in_dim(both, c * SEQ + s, 0, keepdims=False) for c in range(CHUNKS)
    ]
    sent0 = pack(0, arrays)
    in0 = swap(sent0, "seq")
    sent1, in0 = lax.optimization_barrier((pack(1, arrays), in0))
    in1 = swap(sent1, "seq")
    back0, gain0 = attend(0, block_ids, gains[0], in0)
    back0, in1 = lax.optimization_barrier((back0, in1))
    out0 = swap(back0, "seq")
    back1, gain1 = attend(1, block_ids, gains[1], in1)
    part = summed(jnp.concatenate([gain0, gain1], axis=0), "dp", (1, 2, 4))
    back1, part, out0 = lax.optimization_barrier((back1, part, out0))
    out1 = swap(back1, "seq")
    done = unpack(0, out0, ())
    done = unpack(1, out1, tuple(done))
    part = summed(part, "dp", (8,))
    mine = lax.broadcasted_iota(jnp.int32, (SEQ, 1, 1), 0) == s
    every = summed(jnp.where(mine, part[None], 0.0), "seq", (1, 2, 4, 8))
    factor = (TOKENS * lax.axis_size("dp")) ** -0.5
    every = jnp.transpose(every.reshape(SEQ, CHUNKS, 2, HEAD), (2, 1, 0, 3)) * factor
    every = every.reshape(2, HEADS, HEAD)
    return (*done, every[0], every[1])


def solution(mesh):
    rows = P("dp", "seq", None)
    return jax.shard_map(
        on_device,
        mesh=mesh,
        in_specs=(rows, rows, rows, rows, P(), P(), P()),
        out_specs=(rows, rows, rows, rows, P(), P()),
        check_vma=False,
    )
```

```python
import functools

import jax
import jax.numpy as jnp
from jax import lax
from jax.experimental import pallas as pl
from jax.experimental.pallas import tpu as pltpu
from jax.sharding import PartitionSpec as P

HEADS = 32
HEAD = 128
BLOCK = 64
NB = 32
SLOTS = 8
SEQ = 16
CHUNKS = 2
TOK = 128
TOKENS = 2048
EPSILON = 1e-06
SCALE = HEAD**-0.5
LOG2E = 1.4426950408889634
AT_ONCE = 8
EXTRA = 16


def pack_kernel(q_ref, k_ref, v_ref, g_ref, send_ref):
    for a, ref in enumerate((q_ref, k_ref, v_ref, g_ref)):
        for n in range(AT_ONCE):
            send_ref[n, a * TOK : (a + 1) * TOK, :] = ref[0, :, n * HEAD : (n + 1) * HEAD]


def pack(chunk, arrays):
    steps = SEQ // AT_ONCE
    return pl.pallas_call(
        pack_kernel,
        grid=(steps,),
        out_shape=jax.ShapeDtypeStruct((SEQ, 4 * TOK, HEAD), jnp.bfloat16),
        in_specs=[pl.BlockSpec((1, TOK, AT_ONCE * HEAD), lambda i: (0, 0, chunk * steps + i))] * 4,
        out_specs=pl.BlockSpec((AT_ONCE, 4 * TOK, HEAD), lambda i: (i, 0, 0)),
        cost_estimate=pl.CostEstimate(flops=0, bytes_accessed=8 << 20, transcendentals=0),
        name=f"pack{chunk}",
    )(*arrays)


def unpack_kernel(recv_ref, *refs):
    first = pl.program_id(0) * AT_ONCE
    for a, ref in enumerate(refs):
        for n in range(AT_ONCE):
            ref[0, :, n * HEAD : (n + 1) * HEAD] = recv_ref[first + n, a * TOK : (a + 1) * TOK, :]


def last_unpack_kernel(factor, recv_ref, *refs):
    outs, query_gain_ref, key_gain_ref = refs[4:8], refs[8], refs[9]
    first = pl.program_id(0) * AT_ONCE
    for a, ref in enumerate(outs):
        for n in range(AT_ONCE):
            ref[0, :, n * HEAD : (n + 1) * HEAD] = recv_ref[first + n, a * TOK : (a + 1) * TOK, :]

    @pl.when(pl.program_id(0) == 0)
    def _():
        terms = recv_ref[:, 4 * TOK :, :].astype(jnp.float32)
        for c in range(CHUNKS):
            for k, ref in enumerate((query_gain_ref, key_gain_ref)):
                row = 2 * c + k
                total = terms[:, row] + terms[:, 4 + row] + terms[:, 8 + row]
                ref[c * SEQ : (c + 1) * SEQ, :] = total * factor


def unpack(recv):
    steps = SEQ // AT_ONCE
    return pl.pallas_call(
        unpack_kernel,
        grid=(steps,),
        out_shape=(jax.ShapeDtypeStruct((1, TOK, HEADS * HEAD), jnp.bfloat16),) * 4,
        in_specs=[pl.BlockSpec(memory_space=pltpu.VMEM)],
        out_specs=(pl.BlockSpec((1, TOK, AT_ONCE * HEAD), lambda i: (0, 0, i)),) * 4,
        cost_estimate=pl.CostEstimate(flops=0, bytes_accessed=8 << 20, transcendentals=0),
        name="unpack0",
    )(recv)


def last_unpack(factor, recv, before):
    steps = SEQ // AT_ONCE
    gain = jax.ShapeDtypeStruct((HEADS, HEAD), jnp.float32)
    return pl.pallas_call(
        functools.partial(last_unpack_kernel, factor),
        grid=(steps,),
        out_shape=(jax.ShapeDtypeStruct((1, TOK, HEADS * HEAD), jnp.bfloat16),) * 4 + (gain, gain),
        in_specs=[pl.BlockSpec(memory_space=pltpu.VMEM)] + [pl.BlockSpec(memory_space=pl.ANY)] * 4,
        out_specs=(pl.BlockSpec((1, TOK, AT_ONCE * HEAD), lambda i: (0, 0, steps + i)),) * 4
        + (pl.BlockSpec((HEADS, HEAD), lambda i: (0, 0)),) * 2,
        input_output_aliases={i + 1: i for i in range(4)},
        compiler_params=pltpu.CompilerParams(vmem_limit_bytes=24 << 20),
        cost_estimate=pl.CostEstimate(flops=0, bytes_accessed=8 << 20, transcendentals=0),
        name="unpack1",
    )(recv, *before)


def attach_kernel(part_ref, _, send_ref, rows_ref, sem):
    part = part_ref[...]
    high = part.astype(jnp.bfloat16)
    rest = part - high.astype(jnp.float32)
    middle = rest.astype(jnp.bfloat16)
    low = (rest - middle.astype(jnp.float32)).astype(jnp.bfloat16)
    blank = jnp.zeros((EXTRA - 12, HEAD), jnp.bfloat16)
    rows = jnp.concatenate([high, middle, low, blank], axis=0)
    rows_ref[...] = jnp.broadcast_to(rows[None], (SEQ, EXTRA, HEAD))
    copy = pltpu.make_async_copy(rows_ref, send_ref.at[:, pl.ds(4 * TOK, EXTRA), :], sem)
    copy.start()
    copy.wait()


def attach(part, send):
    return pl.pallas_call(
        attach_kernel,
        out_shape=pltpu.HBM(send.shape, send.dtype),
        in_specs=[pl.BlockSpec(memory_space=pltpu.VMEM), pl.BlockSpec(memory_space=pltpu.HBM)],
        out_specs=pl.BlockSpec(memory_space=pltpu.HBM),
        input_output_aliases={1: 0},
        scratch_shapes=[pltpu.VMEM((SEQ, EXTRA, HEAD), jnp.bfloat16), pltpu.SemaphoreType.DMA],
        cost_estimate=pl.CostEstimate(flops=0, bytes_accessed=1 << 17, transcendentals=0),
        name="attach",
    )(part, send)


def dot(a, b, ca, cb):
    return lax.dot_general(
        a, b, (((ca,), (cb,)), ((), ())), preferred_element_type=jnp.float32
    )


def inverse_norm(x):
    return lax.rsqrt(jnp.mean(x * x, axis=-1, keepdims=True) + EPSILON)


def norm_backward(x, inverse, gain, grad):
    unit = x * inverse
    pulled = grad * gain
    along = jnp.mean(pulled * unit, axis=-1, keepdims=True)
    return inverse * (pulled - unit * along), grad * unit


def attend_kernel(
    ids_ref,
    gains_ref,
    recv_ref,
    sent_ref,
    gain_ref,
    back_ref,
    kv_ref,
    qg_ref,
    sum_ref,
    prod_a,
    prod_b,
    mix_a,
    mix_b,
    sems,
    *,
    group,
):
    query_gain = gains_ref[0:1, :]
    key_gain = gains_ref[1:2, :]
    prods, mixes = (prod_a, prod_b), (mix_a, mix_b)
    units = NB // group
    zeros = jnp.zeros((BLOCK, HEAD), jnp.bfloat16)

    @pl.loop(0, SEQ, unroll=4)
    def _(s):
        rows = pl.ds(pl.multiple_of(s * TOK, TOK), TOK)
        x = recv_ref[s, TOK : 2 * TOK, :].astype(jnp.float32)
        kv_ref[rows, :HEAD] = (x * inverse_norm(x) * key_gain).astype(jnp.bfloat16)
        kv_ref[rows, HEAD:] = recv_ref[s, 2 * TOK : 3 * TOK, :]
        sum_ref[rows, :] = jnp.zeros((TOK, 2 * HEAD), jnp.float32)
        x = recv_ref[s, :TOK, :].astype(jnp.float32)
        qn = (x * inverse_norm(x) * query_gain).astype(jnp.bfloat16)
        grad = recv_ref[s, 3 * TOK : 4 * TOK, :]
        for h in range(2):
            part = slice(h * BLOCK, (h + 1) * BLOCK)
            qg_ref[2 * s + h, :BLOCK, :HEAD] = qn[part]
            qg_ref[2 * s + h, :BLOCK, HEAD:] = zeros
            qg_ref[2 * s + h, BLOCK:, :HEAD] = zeros
            qg_ref[2 * s + h, BLOCK:, HEAD:] = grad[part]

    slot_of = lax.broadcasted_iota(jnp.int32, (1, SLOTS * BLOCK), 1) // BLOCK

    def places_of(r):
        blocks = [jnp.maximum(ids_ref[r, j], 0) for j in range(SLOTS)]
        return [pl.ds(pl.multiple_of(b * BLOCK, BLOCK), BLOCK) for b in blocks]

    def near_of(r):
        return jnp.concatenate([kv_ref[p, :] for p in places_of(r)], axis=0)

    def multiply(t, at):
        for n in range(group):
            r = t * group + n
            prods[at][n] = dot(qg_ref[r], near_of(r), 1, 1)

    def weigh(t, at):
        for n in range(group):
            r = t * group + n
            valid = jnp.int32(0)
            for j in range(SLOTS):
                valid = valid | jnp.where(ids_ref[r, j] >= 0, 1 << j, 0)
            bias = jnp.where(((valid >> slot_of) & 1) == 1, 0.0, -1e30)
            grad_probs = prods[at][n, BLOCK:, :]
            raised = jnp.exp2(prods[at][n, :BLOCK, :] * (SCALE * LOG2E) + bias)
            inverse_sum = 1.0 / jnp.sum(raised, axis=-1, keepdims=True)
            delta = jnp.sum(raised * grad_probs, axis=-1, keepdims=True) * inverse_sum
            mixes[at][n, BLOCK:, :] = (raised * inverse_sum).astype(jnp.bfloat16)
            grad_scores = raised * ((grad_probs - delta) * (inverse_sum * SCALE))
            mixes[at][n, :BLOCK, :] = grad_scores.astype(jnp.bfloat16)

    def spread(t, at, total):
        for n in range(group):
            r = t * group + n
            src, first = r // 2, pl.multiple_of((r % 2) * BLOCK, BLOCK)
            mixed = dot(mixes[at][n], near_of(r), 1, 0)
            x = recv_ref[src, pl.ds(first, BLOCK), :].astype(jnp.float32)
            grad_qn = mixed[:BLOCK, :HEAD].astype(jnp.bfloat16).astype(jnp.float32)
            query_grad, gain_term = norm_backward(x, inverse_norm(x), query_gain, grad_qn)
            back_ref[src, pl.ds(first, BLOCK), :] = mixed[BLOCK:, HEAD:].astype(jnp.bfloat16)
            back_ref[src, pl.ds(TOK + first, BLOCK), :] = query_grad.astype(jnp.bfloat16)
            total = total + gain_term.reshape(BLOCK // 8, 8, HEAD).sum(0)
            terms = dot(mixes[at][n], qg_ref[r], 0, 0)
            for j, p in enumerate(places_of(r)):
                sum_ref[p, :] += terms[j * BLOCK : (j + 1) * BLOCK]
        return total

    def step(t, at, total):
        multiply(t, at)
        weigh(t - 1, 1 - at)
        return spread(t - 2, at, total)

    def two_steps(i, total):
        return step(2 * i + 1, 1, step(2 * i, 0, total))

    multiply(0, 0)
    multiply(1, 1)
    weigh(0, 0)
    query_total = lax.fori_loop(1, units // 2, two_steps, jnp.zeros((8, HEAD), jnp.float32))
    weigh(units - 1, 1)
    query_total = spread(units - 2, 0, query_total)
    query_total = spread(units - 1, 1, query_total)

    def leave(half):
        rows = pl.ds(half * 2 * TOK, 2 * TOK)
        return pltpu.make_async_copy(
            back_ref.at[:, rows, :], sent_ref.at[:, rows, :], sems.at[half]
        )

    leave(0).start()

    def finish(s, total):
        rows = pl.ds(pl.multiple_of(s * TOK, TOK), TOK)
        x = recv_ref[s, TOK : 2 * TOK, :].astype(jnp.float32)
        grad_kn = sum_ref[rows, :HEAD].astype(jnp.bfloat16).astype(jnp.float32)
        key_grad, gain_term = norm_backward(x, inverse_norm(x), key_gain, grad_kn)
        back_ref[s, 2 * TOK : 3 * TOK, :] = key_grad.astype(jnp.bfloat16)
        back_ref[s, 3 * TOK : 4 * TOK, :] = sum_ref[rows, HEAD:].astype(jnp.bfloat16)
        return total + gain_term.reshape(TOK // 8, 8, HEAD).sum(0)

    key_total = lax.fori_loop(0, SEQ, finish, jnp.zeros((8, HEAD), jnp.float32), unroll=4)
    leave(1).start()
    gain_ref[0:1, :] = jnp.sum(query_total, axis=0, keepdims=True)
    gain_ref[1:2, :] = jnp.sum(key_total, axis=0, keepdims=True)
    leave(0).wait()
    leave(1).wait()


def attend(chunk, ids, gains, recv, extra=0, group=2):
    return pl.pallas_call(
        functools.partial(attend_kernel, group=group),
        out_shape=(
            pltpu.HBM((SEQ, 4 * TOK + extra, HEAD), jnp.bfloat16),
            jax.ShapeDtypeStruct((2, HEAD), jnp.float32),
        ),
        in_specs=[
            pl.BlockSpec(memory_space=pltpu.SMEM),
            pl.BlockSpec(memory_space=pltpu.VMEM),
            pl.BlockSpec(memory_space=pltpu.VMEM),
        ],
        out_specs=(
            pl.BlockSpec(memory_space=pltpu.HBM),
            pl.BlockSpec(memory_space=pltpu.VMEM),
        ),
        scratch_shapes=[
            pltpu.VMEM((SEQ, 4 * TOK, HEAD), jnp.bfloat16),
            pltpu.VMEM((TOKENS, 2 * HEAD), jnp.bfloat16),
            pltpu.VMEM((NB, 2 * BLOCK, 2 * HEAD), jnp.bfloat16),
            pltpu.VMEM((TOKENS, 2 * HEAD), jnp.float32),
            pltpu.VMEM((group, 2 * BLOCK, SLOTS * BLOCK), jnp.float32),
            pltpu.VMEM((group, 2 * BLOCK, SLOTS * BLOCK), jnp.float32),
            pltpu.VMEM((group, 2 * BLOCK, SLOTS * BLOCK), jnp.bfloat16),
            pltpu.VMEM((group, 2 * BLOCK, SLOTS * BLOCK), jnp.bfloat16),
            pltpu.SemaphoreType.DMA((2,)),
        ],
        compiler_params=pltpu.CompilerParams(vmem_limit_bytes=32 << 20),
        cost_estimate=pl.CostEstimate(
            flops=25_000_000_000,
            bytes_accessed=4 << 20,
            transcendentals=NB * BLOCK * SLOTS * BLOCK,
        ),
        name=f"attend{chunk}",
    )(ids, gains, recv)


def swap(x, axis):
    return lax.all_to_all(x, axis, split_axis=0, concat_axis=0, tiled=True)


def summed(x, axis):
    size, step = lax.axis_size(axis), 1
    while step < size:
        x = x + lax.ppermute(x, axis, [(i, i ^ step) for i in range(size)])
        step *= 2
    return x


def on_device(queries, keys, values, cotangent, query_gain, key_gain, block_ids):
    arrays = (queries, keys, values, cotangent)
    s = lax.axis_index("seq")
    both = jnp.stack([query_gain, key_gain], axis=1)
    gains = [
        lax.dynamic_index_in_dim(both, c * SEQ + s, 0, keepdims=False) for c in range(CHUNKS)
    ]
    sent0 = pack(0, arrays)
    in0 = swap(sent0, "seq")
    sent1, in0 = lax.optimization_barrier((pack(1, arrays), in0))
    in1 = swap(sent1, "seq")
    back0, gain0 = attend(0, block_ids, gains[0], in0)
    back0, in1 = lax.optimization_barrier((back0, in1))
    out0 = swap(back0, "seq")
    back1, gain1 = attend(1, block_ids, gains[1], in1, EXTRA)
    part = summed(jnp.concatenate([gain0, gain1], axis=0), "dp")
    back1 = attach(part, back1)
    out1 = swap(back1, "seq")
    factor = (TOKENS * lax.axis_size("dp")) ** -0.5
    return tuple(last_unpack(factor, out1, unpack(out0)))


def solution(mesh):
    rows = P("dp", "seq", None)
    return jax.shard_map(
        on_device,
        mesh=mesh,
        in_specs=(rows, rows, rows, rows, P(), P(), P()),
        out_specs=(rows, rows, rows, rows, P(), P()),
        check_vma=False,
    )
```

```python
import functools

import jax
import jax.numpy as jnp
from jax import lax
from jax.experimental import pallas as pl
from jax.experimental.pallas import tpu as pltpu
from jax.sharding import PartitionSpec as P

HEADS = 32
HEAD = 128
BLOCK = 64
NB = 32
SLOTS = 8
SEQ = 16
CHUNKS = 2
TOK = 128
TOKENS = 2048
EPSILON = 1e-06
SCALE = HEAD**-0.5
LOG2E = 1.4426950408889634
AT_ONCE = 8
PACKED = 4
EXTRA = 16


def pack_kernel(chunk, q_ref, k_ref, v_ref, g_ref, send_ref, held_ref, in_sems, out_sems):
    def fetch(part):
        for n in range(part * PACKED, (part + 1) * PACKED):
            columns = pl.ds((chunk * SEQ + n) * HEAD, HEAD)
            for a, ref in enumerate((q_ref, k_ref, v_ref, g_ref)):
                pltpu.make_async_copy(
                    ref.at[0, :, columns],
                    held_ref.at[n, pl.ds(a * TOK, TOK), :],
                    in_sems.at[part],
                ).start()

    def whole(part):
        return held_ref.at[pl.ds(part * PACKED, PACKED)]

    def leave(part):
        return pltpu.make_async_copy(
            whole(part), send_ref.at[pl.ds(part * PACKED, PACKED)], out_sems.at[part]
        )

    parts = SEQ // PACKED
    for part in range(parts):
        fetch(part)
    for part in range(parts):
        pltpu.make_async_copy(whole(part), whole(part), in_sems.at[part]).wait()
        leave(part).start()
    for part in range(parts):
        leave(part).wait()


def pack(chunk, arrays):
    parts = SEQ // PACKED
    return pl.pallas_call(
        functools.partial(pack_kernel, chunk),
        out_shape=pltpu.HBM((SEQ, 4 * TOK, HEAD), jnp.bfloat16),
        in_specs=[pl.BlockSpec(memory_space=pl.ANY)] * 4,
        out_specs=pl.BlockSpec(memory_space=pl.ANY),
        scratch_shapes=[
            pltpu.VMEM((SEQ, 4 * TOK, HEAD), jnp.bfloat16),
            pltpu.SemaphoreType.DMA((parts,)),
            pltpu.SemaphoreType.DMA((parts,)),
        ],
        cost_estimate=pl.CostEstimate(flops=0, bytes_accessed=8 << 20, transcendentals=0),
        name=f"pack{chunk}",
    )(*arrays)


def unpack_kernel(recv_ref, *refs):
    first = pl.program_id(0) * AT_ONCE
    for a, ref in enumerate(refs):
        for n in range(AT_ONCE):
            ref[0, :, n * HEAD : (n + 1) * HEAD] = recv_ref[first + n, a * TOK : (a + 1) * TOK, :]


def last_unpack_kernel(factor, recv_ref, *refs):
    outs, query_gain_ref, key_gain_ref = refs[4:8], refs[8], refs[9]
    first = pl.program_id(0) * AT_ONCE
    for a, ref in enumerate(outs):
        for n in range(AT_ONCE):
            ref[0, :, n * HEAD : (n + 1) * HEAD] = recv_ref[first + n, a * TOK : (a + 1) * TOK, :]

    @pl.when(pl.program_id(0) == 0)
    def _():
        terms = recv_ref[:, 4 * TOK :, :].astype(jnp.float32)
        for c in range(CHUNKS):
            for k, ref in enumerate((query_gain_ref, key_gain_ref)):
                row = 2 * c + k
                total = terms[:, row] + terms[:, 4 + row] + terms[:, 8 + row]
                ref[c * SEQ : (c + 1) * SEQ, :] = total * factor


def unpack(recv):
    steps = SEQ // AT_ONCE
    return pl.pallas_call(
        unpack_kernel,
        grid=(steps,),
        out_shape=(jax.ShapeDtypeStruct((1, TOK, HEADS * HEAD), jnp.bfloat16),) * 4,
        in_specs=[pl.BlockSpec(memory_space=pltpu.VMEM)],
        out_specs=(pl.BlockSpec((1, TOK, AT_ONCE * HEAD), lambda i: (0, 0, i)),) * 4,
        cost_estimate=pl.CostEstimate(flops=0, bytes_accessed=8 << 20, transcendentals=0),
        name="unpack0",
    )(recv)


def last_unpack(factor, recv, before):
    steps = SEQ // AT_ONCE
    gain = jax.ShapeDtypeStruct((HEADS, HEAD), jnp.float32)
    return pl.pallas_call(
        functools.partial(last_unpack_kernel, factor),
        grid=(steps,),
        out_shape=(jax.ShapeDtypeStruct((1, TOK, HEADS * HEAD), jnp.bfloat16),) * 4 + (gain, gain),
        in_specs=[pl.BlockSpec(memory_space=pltpu.VMEM)] + [pl.BlockSpec(memory_space=pl.ANY)] * 4,
        out_specs=(pl.BlockSpec((1, TOK, AT_ONCE * HEAD), lambda i: (0, 0, steps + i)),) * 4
        + (pl.BlockSpec((HEADS, HEAD), lambda i: (0, 0)),) * 2,
        input_output_aliases={i + 1: i for i in range(4)},
        compiler_params=pltpu.CompilerParams(vmem_limit_bytes=24 << 20),
        cost_estimate=pl.CostEstimate(flops=0, bytes_accessed=8 << 20, transcendentals=0),
        name="unpack1",
    )(recv, *before)


def attach_kernel(part_ref, other_ref, _, send_ref, rows_ref, sem):
    part = part_ref[...] + other_ref[...]
    high = part.astype(jnp.bfloat16)
    rest = part - high.astype(jnp.float32)
    middle = rest.astype(jnp.bfloat16)
    low = (rest - middle.astype(jnp.float32)).astype(jnp.bfloat16)
    blank = jnp.zeros((EXTRA - 12, HEAD), jnp.bfloat16)
    rows = jnp.concatenate([high, middle, low, blank], axis=0)
    rows_ref[...] = jnp.broadcast_to(rows[None], (SEQ, EXTRA, HEAD))
    copy = pltpu.make_async_copy(rows_ref, send_ref.at[:, pl.ds(4 * TOK, EXTRA), :], sem)
    copy.start()
    copy.wait()


def attach(part, other, send):
    return pl.pallas_call(
        attach_kernel,
        out_shape=pltpu.HBM(send.shape, send.dtype),
        in_specs=[pl.BlockSpec(memory_space=pltpu.VMEM)] * 2
        + [pl.BlockSpec(memory_space=pltpu.HBM)],
        out_specs=pl.BlockSpec(memory_space=pltpu.HBM),
        input_output_aliases={2: 0},
        scratch_shapes=[pltpu.VMEM((SEQ, EXTRA, HEAD), jnp.bfloat16), pltpu.SemaphoreType.DMA],
        compiler_params=pltpu.CompilerParams(vmem_limit_bytes=8 << 20),
        cost_estimate=pl.CostEstimate(flops=0, bytes_accessed=1 << 17, transcendentals=0),
        name="attach",
    )(part, other, send)


def dot(a, b, ca, cb):
    return lax.dot_general(
        a, b, (((ca,), (cb,)), ((), ())), preferred_element_type=jnp.float32
    )


def inverse_norm(x):
    return lax.rsqrt(jnp.mean(x * x, axis=-1, keepdims=True) + EPSILON)


def norm_backward(x, inverse, gain, grad):
    unit = x * inverse
    pulled = grad * gain
    along = jnp.mean(pulled * unit, axis=-1, keepdims=True)
    return inverse * (pulled - unit * along), grad * unit


def attend_kernel(
    ids_ref,
    gains_ref,
    recv_ref,
    sent_ref,
    gain_ref,
    back_ref,
    kv_ref,
    qg_ref,
    sum_ref,
    prod_a,
    prod_b,
    mix_a,
    mix_b,
    sems,
    *,
    group,
):
    query_gain = gains_ref[0:1, :]
    key_gain = gains_ref[1:2, :]
    prods, mixes = (prod_a, prod_b), (mix_a, mix_b)
    units = NB // group
    zeros = jnp.zeros((BLOCK, HEAD), jnp.bfloat16)

    @pl.loop(0, SEQ, unroll=4)
    def _(s):
        rows = pl.ds(pl.multiple_of(s * TOK, TOK), TOK)
        x = recv_ref[s, TOK : 2 * TOK, :].astype(jnp.float32)
        kv_ref[rows, :HEAD] = (x * inverse_norm(x) * key_gain).astype(jnp.bfloat16)
        kv_ref[rows, HEAD:] = recv_ref[s, 2 * TOK : 3 * TOK, :]
        sum_ref[rows, :] = jnp.zeros((TOK, 2 * HEAD), jnp.float32)
        x = recv_ref[s, :TOK, :].astype(jnp.float32)
        qn = (x * inverse_norm(x) * query_gain).astype(jnp.bfloat16)
        grad = recv_ref[s, 3 * TOK : 4 * TOK, :]
        for h in range(2):
            part = slice(h * BLOCK, (h + 1) * BLOCK)
            qg_ref[2 * s + h, :BLOCK, :HEAD] = qn[part]
            qg_ref[2 * s + h, :BLOCK, HEAD:] = zeros
            qg_ref[2 * s + h, BLOCK:, :HEAD] = zeros
            qg_ref[2 * s + h, BLOCK:, HEAD:] = grad[part]

    slot_of = lax.broadcasted_iota(jnp.int32, (1, SLOTS * BLOCK), 1) // BLOCK

    def places_of(r):
        blocks = [jnp.maximum(ids_ref[r, j], 0) for j in range(SLOTS)]
        return [pl.ds(pl.multiple_of(b * BLOCK, BLOCK), BLOCK) for b in blocks]

    def near_of(r):
        return jnp.concatenate([kv_ref[p, :] for p in places_of(r)], axis=0)

    def multiply(t, at):
        for n in range(group):
            r = t * group + n
            prods[at][n] = dot(qg_ref[r], near_of(r), 1, 1)

    def weigh(t, at):
        for n in range(group):
            r = t * group + n
            valid = jnp.int32(0)
            for j in range(SLOTS):
                valid = valid | jnp.where(ids_ref[r, j] >= 0, 1 << j, 0)
            bias = jnp.where(((valid >> slot_of) & 1) == 1, 0.0, -1e30)
            grad_probs = prods[at][n, BLOCK:, :]
            raised = jnp.exp2(prods[at][n, :BLOCK, :] * (SCALE * LOG2E) + bias)
            inverse_sum = 1.0 / jnp.sum(raised, axis=-1, keepdims=True)
            delta = jnp.sum(raised * grad_probs, axis=-1, keepdims=True) * inverse_sum
            mixes[at][n, BLOCK:, :] = (raised * inverse_sum).astype(jnp.bfloat16)
            grad_scores = raised * ((grad_probs - delta) * (inverse_sum * SCALE))
            mixes[at][n, :BLOCK, :] = grad_scores.astype(jnp.bfloat16)

    def spread(t, at, total):
        for n in range(group):
            r = t * group + n
            src, first = r // 2, pl.multiple_of((r % 2) * BLOCK, BLOCK)
            mixed = dot(mixes[at][n], near_of(r), 1, 0)
            x = recv_ref[src, pl.ds(first, BLOCK), :].astype(jnp.float32)
            grad_qn = mixed[:BLOCK, :HEAD].astype(jnp.bfloat16).astype(jnp.float32)
            query_grad, gain_term = norm_backward(x, inverse_norm(x), query_gain, grad_qn)
            back_ref[src, pl.ds(first, BLOCK), :] = mixed[BLOCK:, HEAD:].astype(jnp.bfloat16)
            back_ref[src, pl.ds(TOK + first, BLOCK), :] = query_grad.astype(jnp.bfloat16)
            total = total + gain_term.reshape(BLOCK // 8, 8, HEAD).sum(0)
            terms = dot(mixes[at][n], qg_ref[r], 0, 0)
            for j, p in enumerate(places_of(r)):
                sum_ref[p, :] += terms[j * BLOCK : (j + 1) * BLOCK]
        return total

    def step(t, at, total):
        multiply(t, at)
        weigh(t - 1, 1 - at)
        return spread(t - 2, at, total)

    def two_steps(i, total):
        return step(2 * i + 1, 1, step(2 * i, 0, total))

    multiply(0, 0)
    multiply(1, 1)
    weigh(0, 0)
    query_total = lax.fori_loop(1, units // 2, two_steps, jnp.zeros((8, HEAD), jnp.float32))
    weigh(units - 1, 1)
    query_total = spread(units - 2, 0, query_total)
    query_total = spread(units - 1, 1, query_total)

    def leave(half):
        rows = pl.ds(half * 2 * TOK, 2 * TOK)
        return pltpu.make_async_copy(
            back_ref.at[:, rows, :], sent_ref.at[:, rows, :], sems.at[half]
        )

    leave(0).start()

    def finish(s, total):
        rows = pl.ds(pl.multiple_of(s * TOK, TOK), TOK)
        x = recv_ref[s, TOK : 2 * TOK, :].astype(jnp.float32)
        grad_kn = sum_ref[rows, :HEAD].astype(jnp.bfloat16).astype(jnp.float32)
        key_grad, gain_term = norm_backward(x, inverse_norm(x), key_gain, grad_kn)
        back_ref[s, 2 * TOK : 3 * TOK, :] = key_grad.astype(jnp.bfloat16)
        back_ref[s, 3 * TOK : 4 * TOK, :] = sum_ref[rows, HEAD:].astype(jnp.bfloat16)
        return total + gain_term.reshape(TOK // 8, 8, HEAD).sum(0)

    key_total = lax.fori_loop(0, SEQ, finish, jnp.zeros((8, HEAD), jnp.float32), unroll=4)
    leave(1).start()
    gain_ref[0:1, :] = jnp.sum(query_total, axis=0, keepdims=True)
    gain_ref[1:2, :] = jnp.sum(key_total, axis=0, keepdims=True)
    leave(0).wait()
    leave(1).wait()


def attend(chunk, ids, gains, recv, extra=0, group=2):
    return pl.pallas_call(
        functools.partial(attend_kernel, group=group),
        out_shape=(
            pltpu.HBM((SEQ, 4 * TOK + extra, HEAD), jnp.bfloat16),
            jax.ShapeDtypeStruct((2, HEAD), jnp.float32),
        ),
        in_specs=[
            pl.BlockSpec(memory_space=pltpu.SMEM),
            pl.BlockSpec(memory_space=pltpu.VMEM),
            pl.BlockSpec(memory_space=pltpu.VMEM),
        ],
        out_specs=(
            pl.BlockSpec(memory_space=pltpu.HBM),
            pl.BlockSpec(memory_space=pltpu.VMEM),
        ),
        scratch_shapes=[
            pltpu.VMEM((SEQ, 4 * TOK, HEAD), jnp.bfloat16),
            pltpu.VMEM((TOKENS, 2 * HEAD), jnp.bfloat16),
            pltpu.VMEM((NB, 2 * BLOCK, 2 * HEAD), jnp.bfloat16),
            pltpu.VMEM((TOKENS, 2 * HEAD), jnp.float32),
            pltpu.VMEM((group, 2 * BLOCK, SLOTS * BLOCK), jnp.float32),
            pltpu.VMEM((group, 2 * BLOCK, SLOTS * BLOCK), jnp.float32),
            pltpu.VMEM((group, 2 * BLOCK, SLOTS * BLOCK), jnp.bfloat16),
            pltpu.VMEM((group, 2 * BLOCK, SLOTS * BLOCK), jnp.bfloat16),
            pltpu.SemaphoreType.DMA((2,)),
        ],
        compiler_params=pltpu.CompilerParams(vmem_limit_bytes=32 << 20),
        cost_estimate=pl.CostEstimate(
            flops=25_000_000_000,
            bytes_accessed=4 << 20,
            transcendentals=NB * BLOCK * SLOTS * BLOCK,
        ),
        name=f"attend{chunk}",
    )(ids, gains, recv)


def swap(x, axis):
    return lax.all_to_all(x, axis, split_axis=0, concat_axis=0, tiled=True)


def far(x, axis, step):
    return lax.ppermute(x, axis, [(i, i ^ step) for i in range(lax.axis_size(axis))])


def on_device(queries, keys, values, cotangent, query_gain, key_gain, block_ids):
    arrays = (queries, keys, values, cotangent)
    s = lax.axis_index("seq")
    both = jnp.stack([query_gain, key_gain], axis=1)
    gains = [
        lax.dynamic_index_in_dim(both, c * SEQ + s, 0, keepdims=False) for c in range(CHUNKS)
    ]
    sent0 = pack(0, arrays)
    in0 = swap(sent0, "seq")
    sent1, in0 = lax.optimization_barrier((pack(1, arrays), in0))
    in1 = swap(sent1, "seq")
    back0, gain0 = attend(0, block_ids, gains[0], in0)
    back0, in1 = lax.optimization_barrier((back0, in1))
    out0 = swap(back0, "seq")
    back1, gain1 = attend(1, block_ids, gains[1], in1, EXTRA)
    part = jnp.concatenate([gain0, gain1], axis=0)
    for step in (1, 2, 4):
        part = part + far(part, "dp", step)
    back1 = attach(part, far(part, "dp", 8), back1)
    out1 = swap(back1, "seq")
    factor = (TOKENS * lax.axis_size("dp")) ** -0.5
    return tuple(last_unpack(factor, out1, unpack(out0)))


def solution(mesh):
    rows = P("dp", "seq", None)
    return jax.shard_map(
        on_device,
        mesh=mesh,
        in_specs=(rows, rows, rows, rows, P(), P(), P()),
        out_specs=(rows, rows, rows, rows, P(), P()),
        check_vma=False,
    )
```

```python
import functools

import jax
import jax.numpy as jnp
from jax import lax
from jax.experimental import pallas as pl
from jax.experimental.pallas import tpu as pltpu
from jax.sharding import PartitionSpec as P

HEADS = 32
HEAD = 128
BLOCK = 64
NB = 32
SLOTS = 8
SEQ = 16
CHUNKS = 2
TOK = 128
TOKENS = 2048
EPSILON = 1e-06
SCALE = HEAD**-0.5
LOG2E = 1.4426950408889634
AT_ONCE = 8
PACKED = 4
SIDE = 4


def pack_kernel(chunk, q_ref, k_ref, v_ref, g_ref, send_ref, held_ref, in_sems, out_sems):
    def fetch(part):
        for n in range(part * PACKED, (part + 1) * PACKED):
            columns = pl.ds((chunk * SEQ + n) * HEAD, HEAD)
            for a, ref in enumerate((q_ref, k_ref, v_ref, g_ref)):
                pltpu.make_async_copy(
                    ref.at[0, :, columns],
                    held_ref.at[n, pl.ds(a * TOK, TOK), :],
                    in_sems.at[part],
                ).start()

    def whole(part):
        return held_ref.at[pl.ds(part * PACKED, PACKED)]

    def leave(part):
        return pltpu.make_async_copy(
            whole(part), send_ref.at[pl.ds(part * PACKED, PACKED)], out_sems.at[part]
        )

    parts = SEQ // PACKED
    for part in range(parts):
        fetch(part)
    for part in range(parts):
        pltpu.make_async_copy(whole(part), whole(part), in_sems.at[part]).wait()
        leave(part).start()
    for part in range(parts):
        leave(part).wait()


def pack(chunk, arrays):
    parts = SEQ // PACKED
    return pl.pallas_call(
        functools.partial(pack_kernel, chunk),
        out_shape=pltpu.HBM((SEQ, 4 * TOK, HEAD), jnp.bfloat16),
        in_specs=[pl.BlockSpec(memory_space=pl.ANY)] * 4,
        out_specs=pl.BlockSpec(memory_space=pl.ANY),
        scratch_shapes=[
            pltpu.VMEM((SEQ, 4 * TOK, HEAD), jnp.bfloat16),
            pltpu.SemaphoreType.DMA((parts,)),
            pltpu.SemaphoreType.DMA((parts,)),
        ],
        cost_estimate=pl.CostEstimate(flops=0, bytes_accessed=8 << 20, transcendentals=0),
        name=f"pack{chunk}",
    )(*arrays)


def unpack_kernel(recv_ref, *refs):
    first = pl.program_id(0) * AT_ONCE
    for a, ref in enumerate(refs):
        for n in range(AT_ONCE):
            ref[0, :, n * HEAD : (n + 1) * HEAD] = recv_ref[first + n, a * TOK : (a + 1) * TOK, :]


def last_unpack_kernel(factor, recv_ref, gathered_ref, place_ref, *refs):
    outs, query_gain_ref, key_gain_ref = refs[4:8], refs[8], refs[9]
    first = pl.program_id(0) * AT_ONCE
    for a, ref in enumerate(outs):
        for n in range(AT_ONCE):
            ref[0, :, n * HEAD : (n + 1) * HEAD] = recv_ref[first + n, a * TOK : (a + 1) * TOK, :]

    @pl.when(pl.program_id(0) == 0)
    def _():
        row, column = place_ref[0] // SIDE, place_ref[0] % SIDE
        for x in range(SIDE):
            for y in range(SIDE):
                away = ((row - x + SIDE) % SIDE) * SIDE + (column - y + SIDE) % SIDE
                total = gathered_ref[away] * factor
                for c in range(CHUNKS):
                    head = c * SEQ + x * SIDE + y
                    query_gain_ref[head : head + 1, :] = total[2 * c : 2 * c + 1]
                    key_gain_ref[head : head + 1, :] = total[2 * c + 1 : 2 * c + 2]


def unpack(recv):
    steps = SEQ // AT_ONCE
    return pl.pallas_call(
        unpack_kernel,
        grid=(steps,),
        out_shape=(jax.ShapeDtypeStruct((1, TOK, HEADS * HEAD), jnp.bfloat16),) * 4,
        in_specs=[pl.BlockSpec(memory_space=pltpu.VMEM)],
        out_specs=(pl.BlockSpec((1, TOK, AT_ONCE * HEAD), lambda i: (0, 0, i)),) * 4,
        cost_estimate=pl.CostEstimate(flops=0, bytes_accessed=8 << 20, transcendentals=0),
        name="unpack0",
    )(recv)


def last_unpack(factor, recv, gathered, place, before):
    steps = SEQ // AT_ONCE
    gain = jax.ShapeDtypeStruct((HEADS, HEAD), jnp.float32)
    return pl.pallas_call(
        functools.partial(last_unpack_kernel, factor),
        grid=(steps,),
        out_shape=(jax.ShapeDtypeStruct((1, TOK, HEADS * HEAD), jnp.bfloat16),) * 4 + (gain, gain),
        in_specs=[
            pl.BlockSpec(memory_space=pltpu.VMEM),
            pl.BlockSpec(memory_space=pltpu.VMEM),
            pl.BlockSpec(memory_space=pltpu.SMEM),
        ]
        + [pl.BlockSpec(memory_space=pl.ANY)] * 4,
        out_specs=(pl.BlockSpec((1, TOK, AT_ONCE * HEAD), lambda i: (0, 0, steps + i)),) * 4
        + (pl.BlockSpec((HEADS, HEAD), lambda i: (0, 0)),) * 2,
        input_output_aliases={i + 3: i for i in range(4)},
        compiler_params=pltpu.CompilerParams(vmem_limit_bytes=24 << 20),
        cost_estimate=pl.CostEstimate(flops=0, bytes_accessed=8 << 20, transcendentals=0),
        name="unpack1",
    )(recv, gathered, place, *before)


def dot(a, b, ca, cb):
    return lax.dot_general(
        a, b, (((ca,), (cb,)), ((), ())), preferred_element_type=jnp.float32
    )


def inverse_norm(x):
    return lax.rsqrt(jnp.mean(x * x, axis=-1, keepdims=True) + EPSILON)


def norm_backward(x, inverse, gain, grad):
    unit = x * inverse
    pulled = grad * gain
    along = jnp.mean(pulled * unit, axis=-1, keepdims=True)
    return inverse * (pulled - unit * along), grad * unit


def attend_kernel(
    ids_ref,
    gains_ref,
    recv_ref,
    sent_ref,
    gain_ref,
    back_ref,
    kv_ref,
    qg_ref,
    sum_ref,
    prod_a,
    prod_b,
    mix_a,
    mix_b,
    sems,
    *,
    group,
):
    query_gain = gains_ref[0:1, :]
    key_gain = gains_ref[1:2, :]
    prods, mixes = (prod_a, prod_b), (mix_a, mix_b)
    units = NB // group
    zeros = jnp.zeros((BLOCK, HEAD), jnp.bfloat16)

    @pl.loop(0, SEQ, unroll=4)
    def _(s):
        rows = pl.ds(pl.multiple_of(s * TOK, TOK), TOK)
        x = recv_ref[s, TOK : 2 * TOK, :].astype(jnp.float32)
        kv_ref[rows, :HEAD] = (x * inverse_norm(x) * key_gain).astype(jnp.bfloat16)
        kv_ref[rows, HEAD:] = recv_ref[s, 2 * TOK : 3 * TOK, :]
        sum_ref[rows, :] = jnp.zeros((TOK, 2 * HEAD), jnp.float32)
        x = recv_ref[s, :TOK, :].astype(jnp.float32)
        qn = (x * inverse_norm(x) * query_gain).astype(jnp.bfloat16)
        grad = recv_ref[s, 3 * TOK : 4 * TOK, :]
        for h in range(2):
            part = slice(h * BLOCK, (h + 1) * BLOCK)
            qg_ref[2 * s + h, :BLOCK, :HEAD] = qn[part]
            qg_ref[2 * s + h, :BLOCK, HEAD:] = zeros
            qg_ref[2 * s + h, BLOCK:, :HEAD] = zeros
            qg_ref[2 * s + h, BLOCK:, HEAD:] = grad[part]

    slot_of = lax.broadcasted_iota(jnp.int32, (1, SLOTS * BLOCK), 1) // BLOCK

    def places_of(r):
        blocks = [jnp.maximum(ids_ref[r, j], 0) for j in range(SLOTS)]
        return [pl.ds(pl.multiple_of(b * BLOCK, BLOCK), BLOCK) for b in blocks]

    def near_of(r):
        return jnp.concatenate([kv_ref[p, :] for p in places_of(r)], axis=0)

    def multiply(t, at):
        for n in range(group):
            r = t * group + n
            prods[at][n] = dot(qg_ref[r], near_of(r), 1, 1)

    def weigh(t, at):
        for n in range(group):
            r = t * group + n
            valid = jnp.int32(0)
            for j in range(SLOTS):
                valid = valid | jnp.where(ids_ref[r, j] >= 0, 1 << j, 0)
            bias = jnp.where(((valid >> slot_of) & 1) == 1, 0.0, -1e30)
            grad_probs = prods[at][n, BLOCK:, :]
            raised = jnp.exp2(prods[at][n, :BLOCK, :] * (SCALE * LOG2E) + bias)
            inverse_sum = 1.0 / jnp.sum(raised, axis=-1, keepdims=True)
            delta = jnp.sum(raised * grad_probs, axis=-1, keepdims=True) * inverse_sum
            mixes[at][n, BLOCK:, :] = (raised * inverse_sum).astype(jnp.bfloat16)
            grad_scores = raised * ((grad_probs - delta) * (inverse_sum * SCALE))
            mixes[at][n, :BLOCK, :] = grad_scores.astype(jnp.bfloat16)

    def spread(t, at, total):
        for n in range(group):
            r = t * group + n
            src, first = r // 2, pl.multiple_of((r % 2) * BLOCK, BLOCK)
            mixed = dot(mixes[at][n], near_of(r), 1, 0)
            x = recv_ref[src, pl.ds(first, BLOCK), :].astype(jnp.float32)
            grad_qn = mixed[:BLOCK, :HEAD].astype(jnp.bfloat16).astype(jnp.float32)
            query_grad, gain_term = norm_backward(x, inverse_norm(x), query_gain, grad_qn)
            back_ref[src, pl.ds(first, BLOCK), :] = mixed[BLOCK:, HEAD:].astype(jnp.bfloat16)
            back_ref[src, pl.ds(TOK + first, BLOCK), :] = query_grad.astype(jnp.bfloat16)
            total = total + gain_term.reshape(BLOCK // 8, 8, HEAD).sum(0)
            terms = dot(mixes[at][n], qg_ref[r], 0, 0)
            for j, p in enumerate(places_of(r)):
                sum_ref[p, :] += terms[j * BLOCK : (j + 1) * BLOCK]
        return total

    def step(t, at, total):
        multiply(t, at)
        weigh(t - 1, 1 - at)
        return spread(t - 2, at, total)

    def two_steps(i, total):
        return step(2 * i + 1, 1, step(2 * i, 0, total))

    multiply(0, 0)
    multiply(1, 1)
    weigh(0, 0)
    query_total = lax.fori_loop(1, units // 2, two_steps, jnp.zeros((8, HEAD), jnp.float32))
    weigh(units - 1, 1)
    query_total = spread(units - 2, 0, query_total)
    query_total = spread(units - 1, 1, query_total)

    def leave(half):
        rows = pl.ds(half * 2 * TOK, 2 * TOK)
        return pltpu.make_async_copy(
            back_ref.at[:, rows, :], sent_ref.at[:, rows, :], sems.at[half]
        )

    leave(0).start()

    def finish(s, total):
        rows = pl.ds(pl.multiple_of(s * TOK, TOK), TOK)
        x = recv_ref[s, TOK : 2 * TOK, :].astype(jnp.float32)
        grad_kn = sum_ref[rows, :HEAD].astype(jnp.bfloat16).astype(jnp.float32)
        key_grad, gain_term = norm_backward(x, inverse_norm(x), key_gain, grad_kn)
        back_ref[s, 2 * TOK : 3 * TOK, :] = key_grad.astype(jnp.bfloat16)
        back_ref[s, 3 * TOK : 4 * TOK, :] = sum_ref[rows, HEAD:].astype(jnp.bfloat16)
        return total + gain_term.reshape(TOK // 8, 8, HEAD).sum(0)

    key_total = lax.fori_loop(0, SEQ, finish, jnp.zeros((8, HEAD), jnp.float32), unroll=4)
    leave(1).start()
    gain_ref[0:1, :] = jnp.sum(query_total, axis=0, keepdims=True)
    gain_ref[1:2, :] = jnp.sum(key_total, axis=0, keepdims=True)
    leave(0).wait()
    leave(1).wait()


def attend(chunk, ids, gains, recv, group=2):
    return pl.pallas_call(
        functools.partial(attend_kernel, group=group),
        out_shape=(
            pltpu.HBM((SEQ, 4 * TOK, HEAD), jnp.bfloat16),
            jax.ShapeDtypeStruct((2, HEAD), jnp.float32),
        ),
        in_specs=[
            pl.BlockSpec(memory_space=pltpu.SMEM),
            pl.BlockSpec(memory_space=pltpu.VMEM),
            pl.BlockSpec(memory_space=pltpu.VMEM),
        ],
        out_specs=(
            pl.BlockSpec(memory_space=pltpu.HBM),
            pl.BlockSpec(memory_space=pltpu.VMEM),
        ),
        scratch_shapes=[
            pltpu.VMEM((SEQ, 4 * TOK, HEAD), jnp.bfloat16),
            pltpu.VMEM((TOKENS, 2 * HEAD), jnp.bfloat16),
            pltpu.VMEM((NB, 2 * BLOCK, 2 * HEAD), jnp.bfloat16),
            pltpu.VMEM((TOKENS, 2 * HEAD), jnp.float32),
            pltpu.VMEM((group, 2 * BLOCK, SLOTS * BLOCK), jnp.float32),
            pltpu.VMEM((group, 2 * BLOCK, SLOTS * BLOCK), jnp.float32),
            pltpu.VMEM((group, 2 * BLOCK, SLOTS * BLOCK), jnp.bfloat16),
            pltpu.VMEM((group, 2 * BLOCK, SLOTS * BLOCK), jnp.bfloat16),
            pltpu.SemaphoreType.DMA((2,)),
        ],
        compiler_params=pltpu.CompilerParams(vmem_limit_bytes=32 << 20),
        cost_estimate=pl.CostEstimate(
            flops=25_000_000_000,
            bytes_accessed=4 << 20,
            transcendentals=NB * BLOCK * SLOTS * BLOCK,
        ),
        name=f"attend{chunk}",
    )(ids, gains, recv)


def swap(x, axis):
    return lax.all_to_all(x, axis, split_axis=0, concat_axis=0, tiled=True)


def far(x, axis, step):
    return lax.ppermute(x, axis, [(i, i ^ step) for i in range(lax.axis_size(axis))])


def ring_of(x, stride):
    held = [x]
    for k in range(1, SIDE):
        turn = []
        for i in range(SEQ):
            at = i // stride % SIDE
            turn.append((i, i + ((at + k) % SIDE - at) * stride))
        held.append(lax.ppermute(x, "seq", turn))
    return jnp.stack(held)


def on_device(queries, keys, values, cotangent, query_gain, key_gain, block_ids):
    arrays = (queries, keys, values, cotangent)
    s = lax.axis_index("seq")
    both = jnp.stack([query_gain, key_gain], axis=1)
    gains = [
        lax.dynamic_index_in_dim(both, c * SEQ + s, 0, keepdims=False) for c in range(CHUNKS)
    ]
    sent0 = pack(0, arrays)
    in0 = swap(sent0, "seq")
    sent1, in0 = lax.optimization_barrier((pack(1, arrays), in0))
    in1 = swap(sent1, "seq")
    back0, gain0 = attend(0, block_ids, gains[0], in0)
    back0, in1 = lax.optimization_barrier((back0, in1))
    out0 = swap(back0, "seq")
    back1, gain1 = attend(1, block_ids, gains[1], in1)
    part = ring_of(jnp.concatenate([gain0, gain1], axis=0), 1)
    part, back1, out0 = lax.optimization_barrier((part, back1, out0))
    out1 = swap(back1, "seq")
    for step in (1, 2, 4, 8):
        part = part + far(part, "dp", step)
    part = ring_of(part, SIDE).reshape(SEQ, 2 * CHUNKS, HEAD)
    factor = (TOKENS * lax.axis_size("dp")) ** -0.5
    return tuple(last_unpack(factor, out1, part, s.reshape(1), unpack(out0)))


def solution(mesh):
    rows = P("dp", "seq", None)
    return jax.shard_map(
        on_device,
        mesh=mesh,
        in_specs=(rows, rows, rows, rows, P(), P(), P()),
        out_specs=(rows, rows, rows, rows, P(), P()),
        check_vma=False,
    )
```

```python
import functools

import jax
import jax.numpy as jnp
from jax import lax
from jax.experimental import pallas as pl
from jax.experimental.pallas import tpu as pltpu
from jax.sharding import PartitionSpec as P

HEADS = 32
HEAD = 128
BLOCK = 64
NB = 32
SLOTS = 8
SEQ = 16
CHUNKS = 2
TOK = 128
TOKENS = 2048
EPSILON = 1e-06
SCALE = HEAD**-0.5
LOG2E = 1.4426950408889634
AT_ONCE = 8
PACKED = 4
SIDE = 4


def pack_kernel(chunk, q_ref, k_ref, v_ref, g_ref, send_ref, held_ref, in_sems, out_sems):
    def fetch(part):
        for n in range(part * PACKED, (part + 1) * PACKED):
            columns = pl.ds((chunk * SEQ + n) * HEAD, HEAD)
            for a, ref in enumerate((q_ref, k_ref, v_ref, g_ref)):
                pltpu.make_async_copy(
                    ref.at[0, :, columns],
                    held_ref.at[n, pl.ds(a * TOK, TOK), :],
                    in_sems.at[part],
                ).start()

    def whole(part):
        return held_ref.at[pl.ds(part * PACKED, PACKED)]

    def leave(part):
        return pltpu.make_async_copy(
            whole(part), send_ref.at[pl.ds(part * PACKED, PACKED)], out_sems.at[part]
        )

    parts = SEQ // PACKED
    for part in range(parts):
        fetch(part)
    for part in range(parts):
        pltpu.make_async_copy(whole(part), whole(part), in_sems.at[part]).wait()
        leave(part).start()
    for part in range(parts):
        leave(part).wait()


def pack(chunk, arrays):
    parts = SEQ // PACKED
    return pl.pallas_call(
        functools.partial(pack_kernel, chunk),
        out_shape=pltpu.HBM((SEQ, 4 * TOK, HEAD), jnp.bfloat16),
        in_specs=[pl.BlockSpec(memory_space=pl.ANY)] * 4,
        out_specs=pl.BlockSpec(memory_space=pl.ANY),
        scratch_shapes=[
            pltpu.VMEM((SEQ, 4 * TOK, HEAD), jnp.bfloat16),
            pltpu.SemaphoreType.DMA((parts,)),
            pltpu.SemaphoreType.DMA((parts,)),
        ],
        cost_estimate=pl.CostEstimate(flops=0, bytes_accessed=8 << 20, transcendentals=0),
        name=f"pack{chunk}",
    )(*arrays)


def unpack_kernel(recv_ref, *refs):
    for a, ref in enumerate(refs):
        for n in range(AT_ONCE):
            ref[0, :, n * HEAD : (n + 1) * HEAD] = recv_ref[n, a * TOK : (a + 1) * TOK, :]


def last_unpack_kernel(factor, recv_ref, gathered_ref, place_ref, *refs):
    outs, query_gain_ref, key_gain_ref = refs[4:8], refs[8], refs[9]
    first = pl.program_id(0) * AT_ONCE
    for a, ref in enumerate(outs):
        for n in range(AT_ONCE):
            ref[0, :, n * HEAD : (n + 1) * HEAD] = recv_ref[first + n, a * TOK : (a + 1) * TOK, :]

    @pl.when(pl.program_id(0) == 0)
    def _():
        row, column = place_ref[0] // SIDE, place_ref[0] % SIDE
        for x in range(SIDE):
            for y in range(SIDE):
                away = ((row - x + SIDE) % SIDE) * SIDE + (column - y + SIDE) % SIDE
                total = gathered_ref[away] * factor
                for c in range(CHUNKS):
                    head = c * SEQ + x * SIDE + y
                    query_gain_ref[head : head + 1, :] = total[2 * c : 2 * c + 1]
                    key_gain_ref[head : head + 1, :] = total[2 * c + 1 : 2 * c + 2]


def unpack(recv):
    steps = SEQ // AT_ONCE
    return pl.pallas_call(
        unpack_kernel,
        grid=(steps,),
        out_shape=(jax.ShapeDtypeStruct((1, TOK, HEADS * HEAD), jnp.bfloat16),) * 4,
        in_specs=[pl.BlockSpec((AT_ONCE, 4 * TOK, HEAD), lambda i: (i, 0, 0))],
        out_specs=(pl.BlockSpec((1, TOK, AT_ONCE * HEAD), lambda i: (0, 0, i)),) * 4,
        cost_estimate=pl.CostEstimate(flops=0, bytes_accessed=8 << 20, transcendentals=0),
        name="unpack0",
    )(recv)


def last_unpack(factor, recv, gathered, place, before):
    steps = SEQ // AT_ONCE
    gain = jax.ShapeDtypeStruct((HEADS, HEAD), jnp.float32)
    return pl.pallas_call(
        functools.partial(last_unpack_kernel, factor),
        grid=(steps,),
        out_shape=(jax.ShapeDtypeStruct((1, TOK, HEADS * HEAD), jnp.bfloat16),) * 4 + (gain, gain),
        in_specs=[
            pl.BlockSpec(memory_space=pltpu.VMEM),
            pl.BlockSpec(memory_space=pltpu.VMEM),
            pl.BlockSpec(memory_space=pltpu.SMEM),
        ]
        + [pl.BlockSpec(memory_space=pl.ANY)] * 4,
        out_specs=(pl.BlockSpec((1, TOK, AT_ONCE * HEAD), lambda i: (0, 0, steps + i)),) * 4
        + (pl.BlockSpec((HEADS, HEAD), lambda i: (0, 0)),) * 2,
        input_output_aliases={i + 3: i for i in range(4)},
        compiler_params=pltpu.CompilerParams(vmem_limit_bytes=24 << 20),
        cost_estimate=pl.CostEstimate(flops=0, bytes_accessed=8 << 20, transcendentals=0),
        name="unpack1",
    )(recv, gathered, place, *before)


def dot(a, b, ca, cb):
    return lax.dot_general(
        a, b, (((ca,), (cb,)), ((), ())), preferred_element_type=jnp.float32
    )


def inverse_norm(x):
    return lax.rsqrt(jnp.mean(x * x, axis=-1, keepdims=True) + EPSILON)


def norm_backward(x, inverse, gain, grad):
    unit = x * inverse
    pulled = grad * gain
    along = jnp.mean(pulled * unit, axis=-1, keepdims=True)
    return inverse * (pulled - unit * along), grad * unit


def attend_kernel(
    ids_ref,
    gains_ref,
    recv_ref,
    sent_ref,
    gain_ref,
    back_ref,
    kv_ref,
    qg_ref,
    sum_ref,
    prod_a,
    prod_b,
    mix_a,
    mix_b,
    sems,
    *,
    group,
):
    query_gain = gains_ref[0:1, :]
    key_gain = gains_ref[1:2, :]
    prods, mixes = (prod_a, prod_b), (mix_a, mix_b)
    units = NB // group
    zeros = jnp.zeros((BLOCK, HEAD), jnp.bfloat16)

    @pl.loop(0, SEQ, unroll=4)
    def _(s):
        rows = pl.ds(pl.multiple_of(s * TOK, TOK), TOK)
        x = recv_ref[s, TOK : 2 * TOK, :].astype(jnp.float32)
        kv_ref[rows, :HEAD] = (x * inverse_norm(x) * key_gain).astype(jnp.bfloat16)
        kv_ref[rows, HEAD:] = recv_ref[s, 2 * TOK : 3 * TOK, :]
        sum_ref[rows, :] = jnp.zeros((TOK, 2 * HEAD), jnp.float32)
        x = recv_ref[s, :TOK, :].astype(jnp.float32)
        qn = (x * inverse_norm(x) * query_gain).astype(jnp.bfloat16)
        grad = recv_ref[s, 3 * TOK : 4 * TOK, :]
        for h in range(2):
            part = slice(h * BLOCK, (h + 1) * BLOCK)
            qg_ref[2 * s + h, :BLOCK, :HEAD] = qn[part]
            qg_ref[2 * s + h, :BLOCK, HEAD:] = zeros
            qg_ref[2 * s + h, BLOCK:, :HEAD] = zeros
            qg_ref[2 * s + h, BLOCK:, HEAD:] = grad[part]

    slot_of = lax.broadcasted_iota(jnp.int32, (1, SLOTS * BLOCK), 1) // BLOCK

    def places_of(r):
        blocks = [jnp.maximum(ids_ref[r, j], 0) for j in range(SLOTS)]
        return [pl.ds(pl.multiple_of(b * BLOCK, BLOCK), BLOCK) for b in blocks]

    def near_of(r):
        return jnp.concatenate([kv_ref[p, :] for p in places_of(r)], axis=0)

    def multiply(t, at):
        for n in range(group):
            r = t * group + n
            prods[at][n] = dot(qg_ref[r], near_of(r), 1, 1)

    def weigh(t, at):
        for n in range(group):
            r = t * group + n
            valid = jnp.int32(0)
            for j in range(SLOTS):
                valid = valid | jnp.where(ids_ref[r, j] >= 0, 1 << j, 0)
            bias = jnp.where(((valid >> slot_of) & 1) == 1, 0.0, -1e30)
            grad_probs = prods[at][n, BLOCK:, :]
            raised = jnp.exp2(prods[at][n, :BLOCK, :] * (SCALE * LOG2E) + bias)
            inverse_sum = 1.0 / jnp.sum(raised, axis=-1, keepdims=True)
            delta = jnp.sum(raised * grad_probs, axis=-1, keepdims=True) * inverse_sum
            mixes[at][n, BLOCK:, :] = (raised * inverse_sum).astype(jnp.bfloat16)
            grad_scores = raised * ((grad_probs - delta) * (inverse_sum * SCALE))
            mixes[at][n, :BLOCK, :] = grad_scores.astype(jnp.bfloat16)

    def spread(t, at, total):
        for n in range(group):
            r = t * group + n
            src, first = r // 2, pl.multiple_of((r % 2) * BLOCK, BLOCK)
            mixed = dot(mixes[at][n], near_of(r), 1, 0)
            x = recv_ref[src, pl.ds(first, BLOCK), :].astype(jnp.float32)
            grad_qn = mixed[:BLOCK, :HEAD].astype(jnp.bfloat16).astype(jnp.float32)
            query_grad, gain_term = norm_backward(x, inverse_norm(x), query_gain, grad_qn)
            back_ref[src, pl.ds(first, BLOCK), :] = mixed[BLOCK:, HEAD:].astype(jnp.bfloat16)
            back_ref[src, pl.ds(TOK + first, BLOCK), :] = query_grad.astype(jnp.bfloat16)
            total = total + gain_term.reshape(BLOCK // 8, 8, HEAD).sum(0)
            terms = dot(mixes[at][n], qg_ref[r], 0, 0)
            for j, p in enumerate(places_of(r)):
                sum_ref[p, :] += terms[j * BLOCK : (j + 1) * BLOCK]
        return total

    def step(t, at, total):
        multiply(t, at)
        weigh(t - 1, 1 - at)
        return spread(t - 2, at, total)

    def two_steps(i, total):
        return step(2 * i + 1, 1, step(2 * i, 0, total))

    multiply(0, 0)
    multiply(1, 1)
    weigh(0, 0)
    query_total = lax.fori_loop(1, units // 2, two_steps, jnp.zeros((8, HEAD), jnp.float32))
    weigh(units - 1, 1)
    query_total = spread(units - 2, 0, query_total)
    query_total = spread(units - 1, 1, query_total)

    def leave(half):
        rows = pl.ds(half * 2 * TOK, 2 * TOK)
        return pltpu.make_async_copy(
            back_ref.at[:, rows, :], sent_ref.at[:, rows, :], sems.at[half]
        )

    leave(0).start()

    def finish(s, total):
        rows = pl.ds(pl.multiple_of(s * TOK, TOK), TOK)
        x = recv_ref[s, TOK : 2 * TOK, :].astype(jnp.float32)
        grad_kn = sum_ref[rows, :HEAD].astype(jnp.bfloat16).astype(jnp.float32)
        key_grad, gain_term = norm_backward(x, inverse_norm(x), key_gain, grad_kn)
        back_ref[s, 2 * TOK : 3 * TOK, :] = key_grad.astype(jnp.bfloat16)
        back_ref[s, 3 * TOK : 4 * TOK, :] = sum_ref[rows, HEAD:].astype(jnp.bfloat16)
        return total + gain_term.reshape(TOK // 8, 8, HEAD).sum(0)

    key_total = lax.fori_loop(0, SEQ, finish, jnp.zeros((8, HEAD), jnp.float32), unroll=4)
    leave(1).start()
    gain_ref[0:1, :] = jnp.sum(query_total, axis=0, keepdims=True)
    gain_ref[1:2, :] = jnp.sum(key_total, axis=0, keepdims=True)
    leave(0).wait()
    leave(1).wait()


def attend(chunk, ids, gains, recv, group=2):
    return pl.pallas_call(
        functools.partial(attend_kernel, group=group),
        out_shape=(
            pltpu.HBM((SEQ, 4 * TOK, HEAD), jnp.bfloat16),
            jax.ShapeDtypeStruct((2, HEAD), jnp.float32),
        ),
        in_specs=[
            pl.BlockSpec(memory_space=pltpu.SMEM),
            pl.BlockSpec(memory_space=pltpu.VMEM),
            pl.BlockSpec(memory_space=pltpu.VMEM),
        ],
        out_specs=(
            pl.BlockSpec(memory_space=pltpu.HBM),
            pl.BlockSpec(memory_space=pltpu.VMEM),
        ),
        scratch_shapes=[
            pltpu.VMEM((SEQ, 4 * TOK, HEAD), jnp.bfloat16),
            pltpu.VMEM((TOKENS, 2 * HEAD), jnp.bfloat16),
            pltpu.VMEM((NB, 2 * BLOCK, 2 * HEAD), jnp.bfloat16),
            pltpu.VMEM((TOKENS, 2 * HEAD), jnp.float32),
            pltpu.VMEM((group, 2 * BLOCK, SLOTS * BLOCK), jnp.float32),
            pltpu.VMEM((group, 2 * BLOCK, SLOTS * BLOCK), jnp.float32),
            pltpu.VMEM((group, 2 * BLOCK, SLOTS * BLOCK), jnp.bfloat16),
            pltpu.VMEM((group, 2 * BLOCK, SLOTS * BLOCK), jnp.bfloat16),
            pltpu.SemaphoreType.DMA((2,)),
        ],
        compiler_params=pltpu.CompilerParams(vmem_limit_bytes=(64 if chunk == 0 else 125) << 19),
        cost_estimate=pl.CostEstimate(
            flops=25_000_000_000,
            bytes_accessed=4 << 20,
            transcendentals=NB * BLOCK * SLOTS * BLOCK,
        ),
        name=f"attend{chunk}",
    )(ids, gains, recv)


def swap(x, axis):
    return lax.all_to_all(x, axis, split_axis=0, concat_axis=0, tiled=True)


def far(x, axis, step):
    return lax.ppermute(x, axis, [(i, i ^ step) for i in range(lax.axis_size(axis))])


def ring_of(x, stride):
    held = [x]
    for k in range(1, SIDE):
        turn = []
        for i in range(SEQ):
            at = i // stride % SIDE
            turn.append((i, i + ((at + k) % SIDE - at) * stride))
        held.append(lax.ppermute(x, "seq", turn))
    return jnp.stack(held)


def on_device(queries, keys, values, cotangent, query_gain, key_gain, block_ids):
    arrays = (queries, keys, values, cotangent)
    s = lax.axis_index("seq")
    both = jnp.stack([query_gain, key_gain], axis=1)
    gains = [
        lax.dynamic_index_in_dim(both, c * SEQ + s, 0, keepdims=False) for c in range(CHUNKS)
    ]
    sent0 = pack(0, arrays)
    in0 = swap(sent0, "seq")
    sent1, in0 = lax.optimization_barrier((pack(1, arrays), in0))
    in1 = swap(sent1, "seq")
    back0, gain0 = attend(0, block_ids, gains[0], in0)
    back0, in1 = lax.optimization_barrier((back0, in1))
    out0 = swap(back0, "seq")
    back1, gain1 = attend(1, block_ids, gains[1], in1)
    part = ring_of(jnp.concatenate([gain0, gain1], axis=0), 1)
    part, back1, out0 = lax.optimization_barrier((part, back1, out0))
    out1 = swap(back1, "seq")
    for step in (1, 2, 4, 8):
        part = part + far(part, "dp", step)
    part = ring_of(part, SIDE).reshape(SEQ, 2 * CHUNKS, HEAD)
    factor = (TOKENS * lax.axis_size("dp")) ** -0.5
    return tuple(last_unpack(factor, out1, part, s.reshape(1), unpack(out0)))


def solution(mesh):
    rows = P("dp", "seq", None)
    return jax.shard_map(
        on_device,
        mesh=mesh,
        in_specs=(rows, rows, rows, rows, P(), P(), P()),
        out_specs=(rows, rows, rows, rows, P(), P()),
        check_vma=False,
    )
```

```python
import functools

import jax
import jax.numpy as jnp
from jax import lax
from jax.experimental import pallas as pl
from jax.experimental.pallas import tpu as pltpu
from jax.sharding import PartitionSpec as P

HEADS = 32
HEAD = 128
BLOCK = 64
NB = 32
SLOTS = 8
SEQ = 16
CHUNKS = 2
TOK = 128
TOKENS = 2048
EPSILON = 1e-06
SCALE = HEAD**-0.5
LOG2E = 1.4426950408889634
AT_ONCE = 8
PACKED = 4
SIDE = 4


def pack_kernel(chunk, q_ref, k_ref, v_ref, g_ref, send_ref, held_ref, in_sems, out_sems):
    def fetch(part):
        for n in range(part * PACKED, (part + 1) * PACKED):
            columns = pl.ds((chunk * SEQ + n) * HEAD, HEAD)
            for a, ref in enumerate((q_ref, k_ref, v_ref, g_ref)):
                pltpu.make_async_copy(
                    ref.at[0, :, columns],
                    held_ref.at[n, pl.ds(a * TOK, TOK), :],
                    in_sems.at[part],
                ).start()

    def whole(part):
        return held_ref.at[pl.ds(part * PACKED, PACKED)]

    def leave(part):
        return pltpu.make_async_copy(
            whole(part), send_ref.at[pl.ds(part * PACKED, PACKED)], out_sems.at[part]
        )

    parts = SEQ // PACKED
    for part in range(parts):
        fetch(part)
    for part in range(parts):
        pltpu.make_async_copy(whole(part), whole(part), in_sems.at[part]).wait()
        leave(part).start()
    for part in range(parts):
        leave(part).wait()


def pack(chunk, arrays):
    parts = SEQ // PACKED
    return pl.pallas_call(
        functools.partial(pack_kernel, chunk),
        out_shape=pltpu.HBM((SEQ, 4 * TOK, HEAD), jnp.bfloat16),
        in_specs=[pl.BlockSpec(memory_space=pl.ANY)] * 4,
        out_specs=pl.BlockSpec(memory_space=pl.ANY),
        scratch_shapes=[
            pltpu.VMEM((SEQ, 4 * TOK, HEAD), jnp.bfloat16),
            pltpu.SemaphoreType.DMA((parts,)),
            pltpu.SemaphoreType.DMA((parts,)),
        ],
        cost_estimate=pl.CostEstimate(flops=0, bytes_accessed=8 << 20, transcendentals=0),
        name=f"pack{chunk}",
    )(*arrays)


def unpack_kernel(recv_ref, *refs):
    for a, ref in enumerate(refs):
        for n in range(AT_ONCE):
            ref[0, :, n * HEAD : (n + 1) * HEAD] = recv_ref[n, a * TOK : (a + 1) * TOK, :]


def last_unpack_kernel(factor, recv_ref, gathered_ref, place_ref, *refs):
    outs, query_gain_ref, key_gain_ref = refs[4:8], refs[8], refs[9]
    first = pl.program_id(0) * AT_ONCE
    for a, ref in enumerate(outs):
        for n in range(AT_ONCE):
            ref[0, :, n * HEAD : (n + 1) * HEAD] = recv_ref[first + n, a * TOK : (a + 1) * TOK, :]

    @pl.when(pl.program_id(0) == 0)
    def _():
        row, column = place_ref[0] // SIDE, place_ref[0] % SIDE
        for x in range(SIDE):
            for y in range(SIDE):
                away = ((row - x + SIDE) % SIDE) * SIDE + (column - y + SIDE) % SIDE
                total = gathered_ref[away] * factor
                for c in range(CHUNKS):
                    head = c * SEQ + x * SIDE + y
                    query_gain_ref[head : head + 1, :] = total[2 * c : 2 * c + 1]
                    key_gain_ref[head : head + 1, :] = total[2 * c + 1 : 2 * c + 2]


def unpack(recv):
    steps = SEQ // AT_ONCE
    return pl.pallas_call(
        unpack_kernel,
        grid=(steps,),
        out_shape=(jax.ShapeDtypeStruct((1, TOK, HEADS * HEAD), jnp.bfloat16),) * 4,
        in_specs=[pl.BlockSpec((AT_ONCE, 4 * TOK, HEAD), lambda i: (i, 0, 0))],
        out_specs=(pl.BlockSpec((1, TOK, AT_ONCE * HEAD), lambda i: (0, 0, i)),) * 4,
        cost_estimate=pl.CostEstimate(flops=0, bytes_accessed=8 << 20, transcendentals=0),
        name="unpack0",
    )(recv)


def last_unpack(factor, recv, gathered, place, before):
    steps = SEQ // AT_ONCE
    gain = jax.ShapeDtypeStruct((HEADS, HEAD), jnp.float32)
    return pl.pallas_call(
        functools.partial(last_unpack_kernel, factor),
        grid=(steps,),
        out_shape=(jax.ShapeDtypeStruct((1, TOK, HEADS * HEAD), jnp.bfloat16),) * 4 + (gain, gain),
        in_specs=[
            pl.BlockSpec(memory_space=pltpu.VMEM),
            pl.BlockSpec(memory_space=pltpu.VMEM),
            pl.BlockSpec(memory_space=pltpu.SMEM),
        ]
        + [pl.BlockSpec(memory_space=pl.ANY)] * 4,
        out_specs=(pl.BlockSpec((1, TOK, AT_ONCE * HEAD), lambda i: (0, 0, steps + i)),) * 4
        + (pl.BlockSpec((HEADS, HEAD), lambda i: (0, 0)),) * 2,
        input_output_aliases={i + 3: i for i in range(4)},
        compiler_params=pltpu.CompilerParams(vmem_limit_bytes=24 << 20),
        cost_estimate=pl.CostEstimate(flops=0, bytes_accessed=8 << 20, transcendentals=0),
        name="unpack1",
    )(recv, gathered, place, *before)


def dot(a, b, ca, cb):
    return lax.dot_general(
        a, b, (((ca,), (cb,)), ((), ())), preferred_element_type=jnp.float32
    )


def inverse_norm(x):
    return lax.rsqrt(jnp.mean(x * x, axis=-1, keepdims=True) + EPSILON)


def norm_backward(x, inverse, gain, grad):
    unit = x * inverse
    pulled = grad * gain
    along = jnp.mean(pulled * unit, axis=-1, keepdims=True)
    return inverse * (pulled - unit * along), grad * unit


def attend_kernel(
    ids_ref,
    gains_ref,
    recv_ref,
    sent_ref,
    gain_ref,
    back_ref,
    kv_ref,
    qg_ref,
    sum_ref,
    prod_a,
    prod_b,
    mix_a,
    mix_b,
    sems,
    *,
    group,
):
    query_gain = gains_ref[0:1, :]
    key_gain = gains_ref[1:2, :]
    prods, mixes = (prod_a, prod_b), (mix_a, mix_b)
    units = NB // group
    zeros = jnp.zeros((BLOCK, HEAD), jnp.bfloat16)

    @pl.loop(0, SEQ, unroll=4)
    def _(s):
        rows = pl.ds(pl.multiple_of(s * TOK, TOK), TOK)
        x = recv_ref[s, TOK : 2 * TOK, :].astype(jnp.float32)
        kv_ref[rows, :HEAD] = (x * inverse_norm(x) * key_gain).astype(jnp.bfloat16)
        kv_ref[rows, HEAD:] = recv_ref[s, 2 * TOK : 3 * TOK, :]
        sum_ref[rows, :] = jnp.zeros((TOK, 2 * HEAD), jnp.float32)
        x = recv_ref[s, :TOK, :].astype(jnp.float32)
        qn = (x * inverse_norm(x) * query_gain).astype(jnp.bfloat16)
        grad = recv_ref[s, 3 * TOK : 4 * TOK, :]
        for h in range(2):
            part = slice(h * BLOCK, (h + 1) * BLOCK)
            qg_ref[2 * s + h, :BLOCK, :HEAD] = qn[part]
            qg_ref[2 * s + h, :BLOCK, HEAD:] = zeros
            qg_ref[2 * s + h, BLOCK:, :HEAD] = zeros
            qg_ref[2 * s + h, BLOCK:, HEAD:] = grad[part]

    slot_of = lax.broadcasted_iota(jnp.int32, (1, SLOTS * BLOCK), 1) // BLOCK

    def places_of(r):
        blocks = [jnp.maximum(ids_ref[r, j], 0) for j in range(SLOTS)]
        return [pl.ds(pl.multiple_of(b * BLOCK, BLOCK), BLOCK) for b in blocks]

    def near_of(r):
        return jnp.concatenate([kv_ref[p, :] for p in places_of(r)], axis=0)

    def multiply(t, at):
        for n in range(group):
            r = t * group + n
            prods[at][n] = dot(qg_ref[r], near_of(r), 1, 1)

    def weigh(t, at):
        for n in range(group):
            r = t * group + n
            valid = jnp.int32(0)
            for j in range(SLOTS):
                valid = valid | jnp.where(ids_ref[r, j] >= 0, 1 << j, 0)
            bias = jnp.where(((valid >> slot_of) & 1) == 1, 0.0, -1e30)
            grad_probs = prods[at][n, BLOCK:, :]
            raised = jnp.exp2(prods[at][n, :BLOCK, :] * (SCALE * LOG2E) + bias)
            inverse_sum = 1.0 / jnp.sum(raised, axis=-1, keepdims=True)
            delta = jnp.sum(raised * grad_probs, axis=-1, keepdims=True) * inverse_sum
            mixes[at][n, BLOCK:, :] = (raised * inverse_sum).astype(jnp.bfloat16)
            grad_scores = raised * ((grad_probs - delta) * (inverse_sum * SCALE))
            mixes[at][n, :BLOCK, :] = grad_scores.astype(jnp.bfloat16)

    def spread(t, at, total):
        for n in range(group):
            r = t * group + n
            src, first = r // 2, pl.multiple_of((r % 2) * BLOCK, BLOCK)
            mixed = dot(mixes[at][n], near_of(r), 1, 0)
            x = recv_ref[src, pl.ds(first, BLOCK), :].astype(jnp.float32)
            grad_qn = mixed[:BLOCK, :HEAD].astype(jnp.bfloat16).astype(jnp.float32)
            query_grad, gain_term = norm_backward(x, inverse_norm(x), query_gain, grad_qn)
            back_ref[src, pl.ds(first, BLOCK), :] = mixed[BLOCK:, HEAD:].astype(jnp.bfloat16)
            back_ref[src, pl.ds(TOK + first, BLOCK), :] = query_grad.astype(jnp.bfloat16)
            total = total + gain_term.reshape(BLOCK // 8, 8, HEAD).sum(0)
            terms = dot(mixes[at][n], qg_ref[r], 0, 0)
            for j, p in enumerate(places_of(r)):
                sum_ref[p, :] += terms[j * BLOCK : (j + 1) * BLOCK]
        return total

    def step(t, at, total):
        multiply(t, at)
        weigh(t - 1, 1 - at)
        return spread(t - 2, at, total)

    def two_steps(i, total):
        return step(2 * i + 1, 1, step(2 * i, 0, total))

    multiply(0, 0)
    multiply(1, 1)
    weigh(0, 0)
    query_total = lax.fori_loop(1, units // 2, two_steps, jnp.zeros((8, HEAD), jnp.float32))
    weigh(units - 1, 1)
    query_total = spread(units - 2, 0, query_total)
    query_total = spread(units - 1, 1, query_total)

    def leave(half):
        rows = pl.ds(half * 2 * TOK, 2 * TOK)
        return pltpu.make_async_copy(
            back_ref.at[:, rows, :], sent_ref.at[:, rows, :], sems.at[half]
        )

    leave(0).start()

    def finish(s, total):
        rows = pl.ds(pl.multiple_of(s * TOK, TOK), TOK)
        x = recv_ref[s, TOK : 2 * TOK, :].astype(jnp.float32)
        grad_kn = sum_ref[rows, :HEAD].astype(jnp.bfloat16).astype(jnp.float32)
        key_grad, gain_term = norm_backward(x, inverse_norm(x), key_gain, grad_kn)
        back_ref[s, 2 * TOK : 3 * TOK, :] = key_grad.astype(jnp.bfloat16)
        back_ref[s, 3 * TOK : 4 * TOK, :] = sum_ref[rows, HEAD:].astype(jnp.bfloat16)
        return total + gain_term.reshape(TOK // 8, 8, HEAD).sum(0)

    key_total = lax.fori_loop(0, SEQ, finish, jnp.zeros((8, HEAD), jnp.float32), unroll=4)
    leave(1).start()
    gain_ref[0:1, :] = jnp.sum(query_total, axis=0, keepdims=True)
    gain_ref[1:2, :] = jnp.sum(key_total, axis=0, keepdims=True)
    leave(0).wait()
    leave(1).wait()


def attend(chunk, ids, gains, recv, group=2):
    return pl.pallas_call(
        functools.partial(attend_kernel, group=group),
        out_shape=(
            pltpu.HBM((SEQ, 4 * TOK, HEAD), jnp.bfloat16),
            jax.ShapeDtypeStruct((2, HEAD), jnp.float32),
        ),
        in_specs=[
            pl.BlockSpec(memory_space=pltpu.SMEM),
            pl.BlockSpec(memory_space=pltpu.VMEM),
            pl.BlockSpec(memory_space=pltpu.VMEM),
        ],
        out_specs=(
            pl.BlockSpec(memory_space=pltpu.HBM),
            pl.BlockSpec(memory_space=pltpu.VMEM),
        ),
        scratch_shapes=[
            pltpu.VMEM((SEQ, 4 * TOK, HEAD), jnp.bfloat16),
            pltpu.VMEM((TOKENS, 2 * HEAD), jnp.bfloat16),
            pltpu.VMEM((NB, 2 * BLOCK, 2 * HEAD), jnp.bfloat16),
            pltpu.VMEM((TOKENS, 2 * HEAD), jnp.float32),
            pltpu.VMEM((group, 2 * BLOCK, SLOTS * BLOCK), jnp.float32),
            pltpu.VMEM((group, 2 * BLOCK, SLOTS * BLOCK), jnp.float32),
            pltpu.VMEM((group, 2 * BLOCK, SLOTS * BLOCK), jnp.bfloat16),
            pltpu.VMEM((group, 2 * BLOCK, SLOTS * BLOCK), jnp.bfloat16),
            pltpu.SemaphoreType.DMA((2,)),
        ],
        compiler_params=pltpu.CompilerParams(vmem_limit_bytes=(64 if chunk == 0 else 125) << 19),
        cost_estimate=pl.CostEstimate(
            flops=25_000_000_000,
            bytes_accessed=4 << 20,
            transcendentals=NB * BLOCK * SLOTS * BLOCK,
        ),
        name=f"attend{chunk}",
    )(ids, gains, recv)


def swap(x, axis):
    return lax.all_to_all(x, axis, split_axis=0, concat_axis=0, tiled=True)


def far(x, axis, step):
    return lax.ppermute(x, axis, [(i, i ^ step) for i in range(lax.axis_size(axis))])


def ring_of(x, stride):
    held = [x]
    for k in range(1, SIDE):
        turn = []
        for i in range(SEQ):
            at = i // stride % SIDE
            turn.append((i, i + ((at + k) % SIDE - at) * stride))
        held.append(lax.ppermute(x, "seq", turn))
    return jnp.stack(held)


def on_device(queries, keys, values, cotangent, query_gain, key_gain, block_ids):
    arrays = (queries, keys, values, cotangent)
    s = lax.axis_index("seq")
    both = jnp.stack([query_gain, key_gain], axis=1)
    gains = [
        lax.dynamic_index_in_dim(both, c * SEQ + s, 0, keepdims=False) for c in range(CHUNKS)
    ]
    sent0 = pack(0, arrays)
    in0 = swap(sent0, "seq")
    sent1, in0 = lax.optimization_barrier((pack(1, arrays), in0))
    in1 = swap(sent1, "seq")
    back0, gain0 = attend(0, block_ids, gains[0], in0)
    back0, in1 = lax.optimization_barrier((back0, in1))
    out0 = swap(back0, "seq")
    back1, gain1 = attend(1, block_ids, gains[1], in1)
    part = ring_of(jnp.concatenate([gain0, gain1], axis=0), 1)
    part, back1, out0 = lax.optimization_barrier((part, back1, out0))
    out1 = swap(back1, "seq")
    for step in (1, 2, 4):
        part = part + far(part, "dp", step)
    part, out0 = lax.optimization_barrier((part, out0))
    done, other = lax.optimization_barrier((tuple(unpack(out0)), far(part, "dp", 14)))
    part = ring_of(part + other, SIDE).reshape(SEQ, 2 * CHUNKS, HEAD)
    factor = (TOKENS * lax.axis_size("dp")) ** -0.5
    return tuple(last_unpack(factor, out1, part, s.reshape(1), done))


def solution(mesh):
    rows = P("dp", "seq", None)
    return jax.shard_map(
        on_device,
        mesh=mesh,
        in_specs=(rows, rows, rows, rows, P(), P(), P()),
        out_specs=(rows, rows, rows, rows, P(), P()),
        check_vma=False,
    )
```

```python
import functools

import jax
import jax.numpy as jnp
from jax import lax
from jax.experimental import pallas as pl
from jax.experimental.pallas import tpu as pltpu
from jax.sharding import PartitionSpec as P

HEADS = 32
HEAD = 128
BLOCK = 64
NB = 32
SLOTS = 8
SEQ = 16
CHUNKS = 2
TOK = 128
TOKENS = 2048
EPSILON = 1e-06
SCALE = HEAD**-0.5
LOG2E = 1.4426950408889634
AT_ONCE = 8
PACKED = 4
SIDE = 4


def pack_one(chunk, refs, send_ref, held_ref, in_sems, out_sems):
    parts = SEQ // PACKED

    def whole(part):
        return held_ref.at[pl.ds(part * PACKED, PACKED)]

    def leave(part):
        return pltpu.make_async_copy(
            whole(part), send_ref.at[pl.ds(part * PACKED, PACKED)], out_sems.at[part]
        )

    for part in range(parts):
        for n in range(part * PACKED, (part + 1) * PACKED):
            columns = pl.ds((chunk * SEQ + n) * HEAD, HEAD)
            for a, ref in enumerate(refs):
                pltpu.make_async_copy(
                    ref.at[0, :, columns],
                    held_ref.at[n, pl.ds(a * TOK, TOK), :],
                    in_sems.at[part],
                ).start()
    for part in range(parts):
        pltpu.make_async_copy(whole(part), whole(part), in_sems.at[part]).wait()
        leave(part).start()
    for part in range(parts):
        leave(part).wait()


def pack_first_kernel(core_ref, q_ref, k_ref, v_ref, g_ref, first_ref, second_ref, *scratch):
    refs = (q_ref, k_ref, v_ref, g_ref)

    @pl.when(core_ref[0] == 1)
    def _():
        pack_one(1, refs, second_ref, *scratch)

    pack_one(0, refs, first_ref, *scratch)


def pack_second_kernel(core_ref, q_ref, k_ref, v_ref, g_ref, _, second_ref, *scratch):
    @pl.when(core_ref[0] == 0)
    def _():
        pack_one(1, (q_ref, k_ref, v_ref, g_ref), second_ref, *scratch)


def pack(kernel, outputs, core, *arrays):
    parts = SEQ // PACKED
    some = pl.BlockSpec(memory_space=pl.ANY)
    return pl.pallas_call(
        kernel,
        out_shape=(pltpu.HBM((SEQ, 4 * TOK, HEAD), jnp.bfloat16),) * outputs,
        in_specs=[pl.BlockSpec(memory_space=pltpu.SMEM)] + [some] * len(arrays),
        out_specs=(some,) * outputs,
        input_output_aliases={5: 0} if len(arrays) == 5 else {},
        scratch_shapes=[
            pltpu.VMEM((SEQ, 4 * TOK, HEAD), jnp.bfloat16),
            pltpu.SemaphoreType.DMA((parts,)),
            pltpu.SemaphoreType.DMA((parts,)),
        ],
        cost_estimate=pl.CostEstimate(flops=0, bytes_accessed=8 << 20, transcendentals=0),
        name=f"pack{2 - outputs}",
    )(core, *arrays)


def unpack_kernel(recv_ref, *refs):
    for a, ref in enumerate(refs):
        for n in range(AT_ONCE):
            ref[0, :, n * HEAD : (n + 1) * HEAD] = recv_ref[n, a * TOK : (a + 1) * TOK, :]


def last_unpack_kernel(factor, recv_ref, gathered_ref, place_ref, *refs):
    outs, query_gain_ref, key_gain_ref = refs[4:8], refs[8], refs[9]
    first = pl.program_id(0) * AT_ONCE
    for a, ref in enumerate(outs):
        for n in range(AT_ONCE):
            ref[0, :, n * HEAD : (n + 1) * HEAD] = recv_ref[first + n, a * TOK : (a + 1) * TOK, :]

    @pl.when(pl.program_id(0) == 0)
    def _():
        row, column = place_ref[0] // SIDE, place_ref[0] % SIDE
        for x in range(SIDE):
            for y in range(SIDE):
                away = ((row - x + SIDE) % SIDE) * SIDE + (column - y + SIDE) % SIDE
                total = gathered_ref[away] * factor
                for c in range(CHUNKS):
                    head = c * SEQ + x * SIDE + y
                    query_gain_ref[head : head + 1, :] = total[2 * c : 2 * c + 1]
                    key_gain_ref[head : head + 1, :] = total[2 * c + 1 : 2 * c + 2]


def unpack(recv):
    steps = SEQ // AT_ONCE
    return pl.pallas_call(
        unpack_kernel,
        grid=(steps,),
        out_shape=(jax.ShapeDtypeStruct((1, TOK, HEADS * HEAD), jnp.bfloat16),) * 4,
        in_specs=[pl.BlockSpec((AT_ONCE, 4 * TOK, HEAD), lambda i: (i, 0, 0))],
        out_specs=(pl.BlockSpec((1, TOK, AT_ONCE * HEAD), lambda i: (0, 0, i)),) * 4,
        cost_estimate=pl.CostEstimate(flops=0, bytes_accessed=8 << 20, transcendentals=0),
        name="unpack0",
    )(recv)


def last_unpack(factor, recv, gathered, place, before):
    steps = SEQ // AT_ONCE
    gain = jax.ShapeDtypeStruct((HEADS, HEAD), jnp.float32)
    return pl.pallas_call(
        functools.partial(last_unpack_kernel, factor),
        grid=(steps,),
        out_shape=(jax.ShapeDtypeStruct((1, TOK, HEADS * HEAD), jnp.bfloat16),) * 4 + (gain, gain),
        in_specs=[
            pl.BlockSpec(memory_space=pltpu.VMEM),
            pl.BlockSpec(memory_space=pltpu.VMEM),
            pl.BlockSpec(memory_space=pltpu.SMEM),
        ]
        + [pl.BlockSpec(memory_space=pl.ANY)] * 4,
        out_specs=(pl.BlockSpec((1, TOK, AT_ONCE * HEAD), lambda i: (0, 0, steps + i)),) * 4
        + (pl.BlockSpec((HEADS, HEAD), lambda i: (0, 0)),) * 2,
        input_output_aliases={i + 3: i for i in range(4)},
        compiler_params=pltpu.CompilerParams(vmem_limit_bytes=24 << 20),
        cost_estimate=pl.CostEstimate(flops=0, bytes_accessed=8 << 20, transcendentals=0),
        name="unpack1",
    )(recv, gathered, place, *before)


def dot(a, b, ca, cb):
    return lax.dot_general(
        a, b, (((ca,), (cb,)), ((), ())), preferred_element_type=jnp.float32
    )


def inverse_norm(x):
    return lax.rsqrt(jnp.mean(x * x, axis=-1, keepdims=True) + EPSILON)


def norm_backward(x, inverse, gain, grad):
    unit = x * inverse
    pulled = grad * gain
    along = jnp.mean(pulled * unit, axis=-1, keepdims=True)
    return inverse * (pulled - unit * along), grad * unit


def attend_kernel(
    ids_ref,
    gains_ref,
    recv_ref,
    sent_ref,
    gain_ref,
    back_ref,
    kv_ref,
    qg_ref,
    sum_ref,
    prod_a,
    prod_b,
    mix_a,
    mix_b,
    sems,
    *,
    group,
):
    query_gain = gains_ref[0:1, :]
    key_gain = gains_ref[1:2, :]
    prods, mixes = (prod_a, prod_b), (mix_a, mix_b)
    units = NB // group
    zeros = jnp.zeros((BLOCK, HEAD), jnp.bfloat16)

    @pl.loop(0, SEQ, unroll=4)
    def _(s):
        rows = pl.ds(pl.multiple_of(s * TOK, TOK), TOK)
        x = recv_ref[s, TOK : 2 * TOK, :].astype(jnp.float32)
        kv_ref[rows, :HEAD] = (x * inverse_norm(x) * key_gain).astype(jnp.bfloat16)
        kv_ref[rows, HEAD:] = recv_ref[s, 2 * TOK : 3 * TOK, :]
        sum_ref[rows, :] = jnp.zeros((TOK, 2 * HEAD), jnp.float32)
        x = recv_ref[s, :TOK, :].astype(jnp.float32)
        qn = (x * inverse_norm(x) * query_gain).astype(jnp.bfloat16)
        grad = recv_ref[s, 3 * TOK : 4 * TOK, :]
        for h in range(2):
            part = slice(h * BLOCK, (h + 1) * BLOCK)
            qg_ref[2 * s + h, :BLOCK, :HEAD] = qn[part]
            qg_ref[2 * s + h, :BLOCK, HEAD:] = zeros
            qg_ref[2 * s + h, BLOCK:, :HEAD] = zeros
            qg_ref[2 * s + h, BLOCK:, HEAD:] = grad[part]

    slot_of = lax.broadcasted_iota(jnp.int32, (1, SLOTS * BLOCK), 1) // BLOCK

    def places_of(r):
        blocks = [jnp.maximum(ids_ref[r, j], 0) for j in range(SLOTS)]
        return [pl.ds(pl.multiple_of(b * BLOCK, BLOCK), BLOCK) for b in blocks]

    def near_of(r):
        return jnp.concatenate([kv_ref[p, :] for p in places_of(r)], axis=0)

    def multiply(t, at):
        for n in range(group):
            r = t * group + n
            prods[at][n] = dot(qg_ref[r], near_of(r), 1, 1)

    def weigh(t, at):
        for n in range(group):
            r = t * group + n
            valid = jnp.int32(0)
            for j in range(SLOTS):
                valid = valid | jnp.where(ids_ref[r, j] >= 0, 1 << j, 0)
            bias = jnp.where(((valid >> slot_of) & 1) == 1, 0.0, -1e30)
            grad_probs = prods[at][n, BLOCK:, :]
            raised = jnp.exp2(prods[at][n, :BLOCK, :] * (SCALE * LOG2E) + bias)
            inverse_sum = 1.0 / jnp.sum(raised, axis=-1, keepdims=True)
            delta = jnp.sum(raised * grad_probs, axis=-1, keepdims=True) * inverse_sum
            mixes[at][n, BLOCK:, :] = (raised * inverse_sum).astype(jnp.bfloat16)
            grad_scores = raised * ((grad_probs - delta) * (inverse_sum * SCALE))
            mixes[at][n, :BLOCK, :] = grad_scores.astype(jnp.bfloat16)

    def spread(t, at, total):
        for n in range(group):
            r = t * group + n
            src, first = r // 2, pl.multiple_of((r % 2) * BLOCK, BLOCK)
            mixed = dot(mixes[at][n], near_of(r), 1, 0)
            x = recv_ref[src, pl.ds(first, BLOCK), :].astype(jnp.float32)
            grad_qn = mixed[:BLOCK, :HEAD].astype(jnp.bfloat16).astype(jnp.float32)
            query_grad, gain_term = norm_backward(x, inverse_norm(x), query_gain, grad_qn)
            back_ref[src, pl.ds(first, BLOCK), :] = mixed[BLOCK:, HEAD:].astype(jnp.bfloat16)
            back_ref[src, pl.ds(TOK + first, BLOCK), :] = query_grad.astype(jnp.bfloat16)
            total = total + gain_term.reshape(BLOCK // 8, 8, HEAD).sum(0)
            terms = dot(mixes[at][n], qg_ref[r], 0, 0)
            for j, p in enumerate(places_of(r)):
                sum_ref[p, :] += terms[j * BLOCK : (j + 1) * BLOCK]
        return total

    def step(t, at, total):
        multiply(t, at)
        weigh(t - 1, 1 - at)
        return spread(t - 2, at, total)

    def two_steps(i, total):
        return step(2 * i + 1, 1, step(2 * i, 0, total))

    multiply(0, 0)
    multiply(1, 1)
    weigh(0, 0)
    query_total = lax.fori_loop(1, units // 2, two_steps, jnp.zeros((8, HEAD), jnp.float32))
    weigh(units - 1, 1)
    query_total = spread(units - 2, 0, query_total)
    query_total = spread(units - 1, 1, query_total)

    def leave(half):
        rows = pl.ds(half * 2 * TOK, 2 * TOK)
        return pltpu.make_async_copy(
            back_ref.at[:, rows, :], sent_ref.at[:, rows, :], sems.at[half]
        )

    leave(0).start()

    def finish(s, total):
        rows = pl.ds(pl.multiple_of(s * TOK, TOK), TOK)
        x = recv_ref[s, TOK : 2 * TOK, :].astype(jnp.float32)
        grad_kn = sum_ref[rows, :HEAD].astype(jnp.bfloat16).astype(jnp.float32)
        key_grad, gain_term = norm_backward(x, inverse_norm(x), key_gain, grad_kn)
        back_ref[s, 2 * TOK : 3 * TOK, :] = key_grad.astype(jnp.bfloat16)
        back_ref[s, 3 * TOK : 4 * TOK, :] = sum_ref[rows, HEAD:].astype(jnp.bfloat16)
        return total + gain_term.reshape(TOK // 8, 8, HEAD).sum(0)

    key_total = lax.fori_loop(0, SEQ, finish, jnp.zeros((8, HEAD), jnp.float32), unroll=4)
    leave(1).start()
    gain_ref[0:1, :] = jnp.sum(query_total, axis=0, keepdims=True)
    gain_ref[1:2, :] = jnp.sum(key_total, axis=0, keepdims=True)
    leave(0).wait()
    leave(1).wait()


def attend(chunk, ids, gains, recv, group=2):
    return pl.pallas_call(
        functools.partial(attend_kernel, group=group),
        out_shape=(
            pltpu.HBM((SEQ, 4 * TOK, HEAD), jnp.bfloat16),
            jax.ShapeDtypeStruct((2, HEAD), jnp.float32),
        ),
        in_specs=[
            pl.BlockSpec(memory_space=pltpu.SMEM),
            pl.BlockSpec(memory_space=pltpu.VMEM),
            pl.BlockSpec(memory_space=pltpu.VMEM),
        ],
        out_specs=(
            pl.BlockSpec(memory_space=pltpu.HBM),
            pl.BlockSpec(memory_space=pltpu.VMEM),
        ),
        scratch_shapes=[
            pltpu.VMEM((SEQ, 4 * TOK, HEAD), jnp.bfloat16),
            pltpu.VMEM((TOKENS, 2 * HEAD), jnp.bfloat16),
            pltpu.VMEM((NB, 2 * BLOCK, 2 * HEAD), jnp.bfloat16),
            pltpu.VMEM((TOKENS, 2 * HEAD), jnp.float32),
            pltpu.VMEM((group, 2 * BLOCK, SLOTS * BLOCK), jnp.float32),
            pltpu.VMEM((group, 2 * BLOCK, SLOTS * BLOCK), jnp.float32),
            pltpu.VMEM((group, 2 * BLOCK, SLOTS * BLOCK), jnp.bfloat16),
            pltpu.VMEM((group, 2 * BLOCK, SLOTS * BLOCK), jnp.bfloat16),
            pltpu.SemaphoreType.DMA((2,)),
        ],
        compiler_params=pltpu.CompilerParams(vmem_limit_bytes=(64 if chunk == 0 else 125) << 19),
        cost_estimate=pl.CostEstimate(
            flops=25_000_000_000,
            bytes_accessed=4 << 20,
            transcendentals=NB * BLOCK * SLOTS * BLOCK,
        ),
        name=f"attend{chunk}",
    )(ids, gains, recv)


def swap(x, axis):
    return lax.all_to_all(x, axis, split_axis=0, concat_axis=0, tiled=True)


def far(x, axis, step):
    return lax.ppermute(x, axis, [(i, i ^ step) for i in range(lax.axis_size(axis))])


def ring_of(x, stride):
    held = [x]
    for k in range(1, SIDE):
        turn = []
        for i in range(SEQ):
            at = i // stride % SIDE
            turn.append((i, i + ((at + k) % SIDE - at) * stride))
        held.append(lax.ppermute(x, "seq", turn))
    return jnp.stack(held)


def on_device(queries, keys, values, cotangent, query_gain, key_gain, block_ids):
    arrays = (queries, keys, values, cotangent)
    s = lax.axis_index("seq")
    both = jnp.stack([query_gain, key_gain], axis=1)
    gains = [
        lax.dynamic_index_in_dim(both, c * SEQ + s, 0, keepdims=False) for c in range(CHUNKS)
    ]
    core = (lax.axis_index("dp") % 2).reshape(1)
    sent0, sent1 = pack(pack_first_kernel, 2, core, *arrays)
    in0 = swap(sent0, "seq")
    (sent1,) = pack(pack_second_kernel, 1, core, *arrays, sent1)
    sent1, in0 = lax.optimization_barrier((sent1, in0))
    in1 = swap(sent1, "seq")
    back0, gain0 = attend(0, block_ids, gains[0], in0)
    back0, in1 = lax.optimization_barrier((back0, in1))
    out0 = swap(back0, "seq")
    back1, gain1 = attend(1, block_ids, gains[1], in1)
    part = ring_of(jnp.concatenate([gain0, gain1], axis=0), 1)
    part, back1, out0 = lax.optimization_barrier((part, back1, out0))
    out1 = swap(back1, "seq")
    for step in (1, 2, 4):
        part = part + far(part, "dp", step)
    part, out0 = lax.optimization_barrier((part, out0))
    done, other = lax.optimization_barrier((tuple(unpack(out0)), far(part, "dp", 14)))
    part = ring_of(part + other, SIDE).reshape(SEQ, 2 * CHUNKS, HEAD)
    factor = (TOKENS * lax.axis_size("dp")) ** -0.5
    return tuple(last_unpack(factor, out1, part, s.reshape(1), done))


def solution(mesh):
    rows = P("dp", "seq", None)
    return jax.shard_map(
        on_device,
        mesh=mesh,
        in_specs=(rows, rows, rows, rows, P(), P(), P()),
        out_specs=(rows, rows, rows, rows, P(), P()),
        check_vma=False,
    )
```

```python
import functools

import jax
import jax.numpy as jnp
from jax import lax
from jax.experimental import pallas as pl
from jax.experimental.pallas import tpu as pltpu
from jax.sharding import PartitionSpec as P

HEADS = 32
HEAD = 128
BLOCK = 64
NB = 32
SLOTS = 8
SEQ = 16
CHUNKS = 2
TOK = 128
TOKENS = 2048
EPSILON = 1e-06
SCALE = HEAD**-0.5
LOG2E = 1.4426950408889634
AT_ONCE = 8
PACKED = 4
SIDE = 4


def pack_one(chunk, refs, send_ref, held_ref, in_sems, out_sems):
    parts = SEQ // PACKED

    def whole(part):
        return held_ref.at[pl.ds(part * PACKED, PACKED)]

    def leave(part):
        return pltpu.make_async_copy(
            whole(part), send_ref.at[pl.ds(part * PACKED, PACKED)], out_sems.at[part]
        )

    for part in range(parts):
        for n in range(part * PACKED, (part + 1) * PACKED):
            columns = pl.ds((chunk * SEQ + n) * HEAD, HEAD)
            for a, ref in enumerate(refs):
                pltpu.make_async_copy(
                    ref.at[0, :, columns],
                    held_ref.at[n, pl.ds(a * TOK, TOK), :],
                    in_sems.at[part],
                ).start()
    for part in range(parts):
        pltpu.make_async_copy(whole(part), whole(part), in_sems.at[part]).wait()
        leave(part).start()
    for part in range(parts):
        leave(part).wait()


def pack_first_kernel(core_ref, q_ref, k_ref, v_ref, g_ref, first_ref, second_ref, *scratch):
    refs = (q_ref, k_ref, v_ref, g_ref)

    @pl.when(core_ref[0] == 1)
    def _():
        pack_one(1, refs, second_ref, *scratch)

    pack_one(0, refs, first_ref, *scratch)


def pack_second_kernel(core_ref, q_ref, k_ref, v_ref, g_ref, _, second_ref, *scratch):
    @pl.when(core_ref[0] == 0)
    def _():
        pack_one(1, (q_ref, k_ref, v_ref, g_ref), second_ref, *scratch)


def pack(kernel, outputs, core, *arrays):
    parts = SEQ // PACKED
    some = pl.BlockSpec(memory_space=pl.ANY)
    return pl.pallas_call(
        kernel,
        out_shape=(pltpu.HBM((SEQ, 4 * TOK, HEAD), jnp.bfloat16),) * outputs,
        in_specs=[pl.BlockSpec(memory_space=pltpu.SMEM)] + [some] * len(arrays),
        out_specs=(some,) * outputs,
        input_output_aliases={5: 0} if len(arrays) == 5 else {},
        scratch_shapes=[
            pltpu.VMEM((SEQ, 4 * TOK, HEAD), jnp.bfloat16),
            pltpu.SemaphoreType.DMA((parts,)),
            pltpu.SemaphoreType.DMA((parts,)),
        ],
        cost_estimate=pl.CostEstimate(flops=0, bytes_accessed=8 << 20, transcendentals=0),
        name=f"pack{2 - outputs}",
    )(core, *arrays)


def unpack_kernel(recv_ref, *refs):
    for a, ref in enumerate(refs):
        for n in range(AT_ONCE):
            ref[0, :, n * HEAD : (n + 1) * HEAD] = recv_ref[n, a * TOK : (a + 1) * TOK, :]


def last_unpack_kernel(factor, recv_ref, gathered_ref, place_ref, *refs):
    outs, query_gain_ref, key_gain_ref = refs[4:8], refs[8], refs[9]
    first = pl.program_id(0) * AT_ONCE
    for a, ref in enumerate(outs):
        for n in range(AT_ONCE):
            ref[0, :, n * HEAD : (n + 1) * HEAD] = recv_ref[first + n, a * TOK : (a + 1) * TOK, :]

    @pl.when(pl.program_id(0) == 0)
    def _():
        row, column = place_ref[0] // SIDE, place_ref[0] % SIDE
        for x in range(SIDE):
            for y in range(SIDE):
                away = ((row - x + SIDE) % SIDE) * SIDE + (column - y + SIDE) % SIDE
                total = gathered_ref[away] * factor
                for c in range(CHUNKS):
                    head = c * SEQ + x * SIDE + y
                    query_gain_ref[head : head + 1, :] = total[2 * c : 2 * c + 1]
                    key_gain_ref[head : head + 1, :] = total[2 * c + 1 : 2 * c + 2]


def unpack(recv):
    steps = SEQ // AT_ONCE
    return pl.pallas_call(
        unpack_kernel,
        grid=(steps,),
        out_shape=(jax.ShapeDtypeStruct((1, TOK, HEADS * HEAD), jnp.bfloat16),) * 4,
        in_specs=[pl.BlockSpec((AT_ONCE, 4 * TOK, HEAD), lambda i: (i, 0, 0))],
        out_specs=(pl.BlockSpec((1, TOK, AT_ONCE * HEAD), lambda i: (0, 0, i)),) * 4,
        cost_estimate=pl.CostEstimate(flops=0, bytes_accessed=8 << 20, transcendentals=0),
        name="unpack0",
    )(recv)


def last_unpack(factor, recv, gathered, place, before):
    steps = SEQ // AT_ONCE
    gain = jax.ShapeDtypeStruct((HEADS, HEAD), jnp.float32)
    return pl.pallas_call(
        functools.partial(last_unpack_kernel, factor),
        grid=(steps,),
        out_shape=(jax.ShapeDtypeStruct((1, TOK, HEADS * HEAD), jnp.bfloat16),) * 4 + (gain, gain),
        in_specs=[
            pl.BlockSpec(memory_space=pltpu.VMEM),
            pl.BlockSpec(memory_space=pltpu.VMEM),
            pl.BlockSpec(memory_space=pltpu.SMEM),
        ]
        + [pl.BlockSpec(memory_space=pl.ANY)] * 4,
        out_specs=(pl.BlockSpec((1, TOK, AT_ONCE * HEAD), lambda i: (0, 0, steps + i)),) * 4
        + (pl.BlockSpec((HEADS, HEAD), lambda i: (0, 0)),) * 2,
        input_output_aliases={i + 3: i for i in range(4)},
        compiler_params=pltpu.CompilerParams(vmem_limit_bytes=24 << 20),
        cost_estimate=pl.CostEstimate(flops=0, bytes_accessed=8 << 20, transcendentals=0),
        name="unpack1",
    )(recv, gathered, place, *before)


def dot(a, b, ca, cb):
    return lax.dot_general(
        a, b, (((ca,), (cb,)), ((), ())), preferred_element_type=jnp.float32
    )


def inverse_norm(x):
    return lax.rsqrt(jnp.mean(x * x, axis=-1, keepdims=True) + EPSILON)


def norm_backward(x, inverse, gain, grad):
    unit = x * inverse
    pulled = grad * gain
    along = jnp.mean(pulled * unit, axis=-1, keepdims=True)
    return inverse * (pulled - unit * along), grad * unit


def attend_kernel(
    ids_ref,
    gains_ref,
    recv_ref,
    sent_ref,
    gain_ref,
    back_ref,
    kv_ref,
    qg_ref,
    sum_ref,
    prod_a,
    prod_b,
    mix_a,
    mix_b,
    sems,
    *,
    group,
):
    query_gain = gains_ref[0:1, :]
    key_gain = gains_ref[1:2, :]
    prods, mixes = (prod_a, prod_b), (mix_a, mix_b)
    units = NB // group
    zeros = jnp.zeros((BLOCK, HEAD), jnp.bfloat16)

    @pl.loop(0, SEQ, unroll=4)
    def _(s):
        rows = pl.ds(pl.multiple_of(s * TOK, TOK), TOK)
        x = recv_ref[s, TOK : 2 * TOK, :].astype(jnp.float32)
        kv_ref[rows, :HEAD] = (x * inverse_norm(x) * key_gain).astype(jnp.bfloat16)
        kv_ref[rows, HEAD:] = recv_ref[s, 2 * TOK : 3 * TOK, :]
        sum_ref[rows, :] = jnp.zeros((TOK, 2 * HEAD), jnp.float32)
        x = recv_ref[s, :TOK, :].astype(jnp.float32)
        qn = (x * inverse_norm(x) * query_gain).astype(jnp.bfloat16)
        grad = recv_ref[s, 3 * TOK : 4 * TOK, :]
        for h in range(2):
            part = slice(h * BLOCK, (h + 1) * BLOCK)
            qg_ref[2 * s + h, :BLOCK, :HEAD] = qn[part]
            qg_ref[2 * s + h, :BLOCK, HEAD:] = zeros
            qg_ref[2 * s + h, BLOCK:, :HEAD] = zeros
            qg_ref[2 * s + h, BLOCK:, HEAD:] = grad[part]

    slot_of = lax.broadcasted_iota(jnp.int32, (1, SLOTS * BLOCK), 1) // BLOCK

    def places_of(r):
        blocks = [jnp.maximum(ids_ref[r, j], 0) for j in range(SLOTS)]
        return [pl.ds(pl.multiple_of(b * BLOCK, BLOCK), BLOCK) for b in blocks]

    def near_of(r):
        return jnp.concatenate([kv_ref[p, :] for p in places_of(r)], axis=0)

    def multiply(t, at):
        for n in range(group):
            r = t * group + n
            prods[at][n] = dot(qg_ref[r], near_of(r), 1, 1)

    def weigh(t, at):
        for n in range(group):
            r = t * group + n
            valid = jnp.int32(0)
            for j in range(SLOTS):
                valid = valid | jnp.where(ids_ref[r, j] >= 0, 1 << j, 0)
            bias = jnp.where(((valid >> slot_of) & 1) == 1, 0.0, -1e30)
            grad_probs = prods[at][n, BLOCK:, :]
            raised = jnp.exp2(prods[at][n, :BLOCK, :] * (SCALE * LOG2E) + bias)
            inverse_sum = 1.0 / jnp.sum(raised, axis=-1, keepdims=True)
            delta = jnp.sum(raised * grad_probs, axis=-1, keepdims=True) * inverse_sum
            mixes[at][n, BLOCK:, :] = (raised * inverse_sum).astype(jnp.bfloat16)
            grad_scores = raised * ((grad_probs - delta) * (inverse_sum * SCALE))
            mixes[at][n, :BLOCK, :] = grad_scores.astype(jnp.bfloat16)

    def spread(t, at, total):
        for n in range(group):
            r = t * group + n
            src, first = r // 2, pl.multiple_of((r % 2) * BLOCK, BLOCK)
            mixed = dot(mixes[at][n], near_of(r), 1, 0)
            x = recv_ref[src, pl.ds(first, BLOCK), :].astype(jnp.float32)
            grad_qn = mixed[:BLOCK, :HEAD].astype(jnp.bfloat16).astype(jnp.float32)
            query_grad, gain_term = norm_backward(x, inverse_norm(x), query_gain, grad_qn)
            back_ref[src, pl.ds(first, BLOCK), :] = mixed[BLOCK:, HEAD:].astype(jnp.bfloat16)
            back_ref[src, pl.ds(TOK + first, BLOCK), :] = query_grad.astype(jnp.bfloat16)
            total = total + gain_term.reshape(BLOCK // 8, 8, HEAD).sum(0)
            terms = dot(mixes[at][n], qg_ref[r], 0, 0)
            for j, p in enumerate(places_of(r)):
                sum_ref[p, :] += terms[j * BLOCK : (j + 1) * BLOCK]
        return total

    def step(t, at, total):
        multiply(t, at)
        weigh(t - 1, 1 - at)
        return spread(t - 2, at, total)

    def two_steps(i, total):
        return step(2 * i + 1, 1, step(2 * i, 0, total))

    multiply(0, 0)
    multiply(1, 1)
    weigh(0, 0)
    query_total = lax.fori_loop(1, units // 2, two_steps, jnp.zeros((8, HEAD), jnp.float32))
    weigh(units - 1, 1)
    query_total = spread(units - 2, 0, query_total)
    query_total = spread(units - 1, 1, query_total)

    def leave(half):
        rows = pl.ds(half * 2 * TOK, 2 * TOK)
        return pltpu.make_async_copy(
            back_ref.at[:, rows, :], sent_ref.at[:, rows, :], sems.at[half]
        )

    leave(0).start()

    def finish(s, total):
        rows = pl.ds(pl.multiple_of(s * TOK, TOK), TOK)
        x = recv_ref[s, TOK : 2 * TOK, :].astype(jnp.float32)
        grad_kn = sum_ref[rows, :HEAD].astype(jnp.bfloat16).astype(jnp.float32)
        key_grad, gain_term = norm_backward(x, inverse_norm(x), key_gain, grad_kn)
        back_ref[s, 2 * TOK : 3 * TOK, :] = key_grad.astype(jnp.bfloat16)
        back_ref[s, 3 * TOK : 4 * TOK, :] = sum_ref[rows, HEAD:].astype(jnp.bfloat16)
        return total + gain_term.reshape(TOK // 8, 8, HEAD).sum(0)

    key_total = lax.fori_loop(0, SEQ, finish, jnp.zeros((8, HEAD), jnp.float32), unroll=4)
    leave(1).start()
    gain_ref[0:1, :] = jnp.sum(query_total, axis=0, keepdims=True)
    gain_ref[1:2, :] = jnp.sum(key_total, axis=0, keepdims=True)
    leave(0).wait()
    leave(1).wait()


def attend(chunk, ids, gains, recv, group=2):
    return pl.pallas_call(
        functools.partial(attend_kernel, group=group),
        out_shape=(
            pltpu.HBM((SEQ, 4 * TOK, HEAD), jnp.bfloat16),
            jax.ShapeDtypeStruct((2, HEAD), jnp.float32),
        ),
        in_specs=[
            pl.BlockSpec(memory_space=pltpu.SMEM),
            pl.BlockSpec(memory_space=pltpu.VMEM),
            pl.BlockSpec(memory_space=pltpu.VMEM),
        ],
        out_specs=(
            pl.BlockSpec(memory_space=pltpu.HBM),
            pl.BlockSpec(memory_space=pltpu.VMEM),
        ),
        scratch_shapes=[
            pltpu.VMEM((SEQ, 4 * TOK, HEAD), jnp.bfloat16),
            pltpu.VMEM((TOKENS, 2 * HEAD), jnp.bfloat16),
            pltpu.VMEM((NB, 2 * BLOCK, 2 * HEAD), jnp.bfloat16),
            pltpu.VMEM((TOKENS, 2 * HEAD), jnp.float32),
            pltpu.VMEM((group, 2 * BLOCK, SLOTS * BLOCK), jnp.float32),
            pltpu.VMEM((group, 2 * BLOCK, SLOTS * BLOCK), jnp.float32),
            pltpu.VMEM((group, 2 * BLOCK, SLOTS * BLOCK), jnp.bfloat16),
            pltpu.VMEM((group, 2 * BLOCK, SLOTS * BLOCK), jnp.bfloat16),
            pltpu.SemaphoreType.DMA((2,)),
        ],
        compiler_params=pltpu.CompilerParams(vmem_limit_bytes=(64 if chunk == 0 else 125) << 19),
        cost_estimate=pl.CostEstimate(
            flops=25_000_000_000,
            bytes_accessed=4 << 20,
            transcendentals=NB * BLOCK * SLOTS * BLOCK,
        ),
        name=f"attend{chunk}",
    )(ids, gains, recv)


def swap(x, axis):
    return lax.all_to_all(x, axis, split_axis=0, concat_axis=0, tiled=True)


def far(x, axis, step):
    return lax.ppermute(x, axis, [(i, i ^ step) for i in range(lax.axis_size(axis))])


def ring_of(x, stride):
    held = [x]
    for k in range(1, SIDE):
        turn = []
        for i in range(SEQ):
            at = i // stride % SIDE
            turn.append((i, i + ((at + k) % SIDE - at) * stride))
        held.append(lax.ppermute(x, "seq", turn))
    return jnp.stack(held)


def on_device(queries, keys, values, cotangent, query_gain, key_gain, block_ids):
    arrays = (queries, keys, values, cotangent)
    s = lax.axis_index("seq")
    both = jnp.stack([query_gain, key_gain], axis=1)
    gains = [
        lax.dynamic_index_in_dim(both, c * SEQ + s, 0, keepdims=False) for c in range(CHUNKS)
    ]
    core = ((lax.axis_index("dp") + 1) % 2).reshape(1)
    sent0, sent1 = pack(pack_first_kernel, 2, core, *arrays)
    in0 = swap(sent0, "seq")
    (sent1,) = pack(pack_second_kernel, 1, core, *arrays, sent1)
    sent1, in0 = lax.optimization_barrier((sent1, in0))
    in1 = swap(sent1, "seq")
    back0, gain0 = attend(0, block_ids, gains[0], in0)
    back0, in1 = lax.optimization_barrier((back0, in1))
    out0 = swap(back0, "seq")
    back1, gain1 = attend(1, block_ids, gains[1], in1)
    part = ring_of(jnp.concatenate([gain0, gain1], axis=0), 1)
    part, back1, out0 = lax.optimization_barrier((part, back1, out0))
    out1 = swap(back1, "seq")
    for step in (1, 2, 4):
        part = part + far(part, "dp", step)
    part, out0 = lax.optimization_barrier((part, out0))
    done, other = lax.optimization_barrier((tuple(unpack(out0)), far(part, "dp", 14)))
    part = ring_of(part + other, SIDE).reshape(SEQ, 2 * CHUNKS, HEAD)
    factor = (TOKENS * lax.axis_size("dp")) ** -0.5
    return tuple(last_unpack(factor, out1, part, s.reshape(1), done))


def solution(mesh):
    rows = P("dp", "seq", None)
    return jax.shard_map(
        on_device,
        mesh=mesh,
        in_specs=(rows, rows, rows, rows, P(), P(), P()),
        out_specs=(rows, rows, rows, rows, P(), P()),
        check_vma=False,
    )
```
